128 devices in a mesh: dp: 4 (over x), seq: 16 (over z, y), tensor: 2 (over core).
Axes of the slice: x: 4, y: 4, z: 4, core: 2. Of those that a mesh axis runs over, the one named last changes fastest.
Arguments:
- queries: bfloat16 [8192, 4096], P(('dp', 'seq'), 'tensor'), may hold values from -6 to 6
- keys: bfloat16 [8192, 512], P(('dp', 'seq'), 'tensor'), may hold values from -6 to 6
- values: bfloat16 [8192, 512], P(('dp', 'seq'), 'tensor'), may hold values from -6 to 6
- out_weight: bfloat16 [4096, 8192], P('tensor', 'seq'), may hold values from -0.09375 to 0.09375
- doc_len: int32 [4, 16], P('dp'), may hold values from 1 to 1024, as said below
- destination: int32 [4, 16], P('dp'), may hold values from 0 to 3, as said below
Outputs:
- attended: bfloat16 [16384, 8192], P(('dp', 'tensor'), 'seq')
The draws below stay inside these ranges and needn't reach their ends.
Inputs may be any that keep to these rules, and one draw needn't show every extreme that they name: `doc_len`: each row sums to 2048; in each row one document has exactly 1024 tokens. destination[g, j] is g or g XOR (2).
All inputs are finite; a program needn't handle non-finite values.
Results may differ from the reference program's by a relative error of at most 0.0095.
Values may be sent and summed in bfloat16 or wider, within the bound.
A program may use at most 192 MiB of HBM per device.

```python
import math
import jax
import jax.numpy as jnp
from jax import lax

D = 8192
QUERY_HEADS = 32
KEY_VALUE_HEADS = 4
HEAD_SIZE = 128
DOCS = 16
TOK_DEV = 128
GROUPS = 4
SLAB = 2048
SLOTS = 4096
TOKEN_TOTAL = 8192
N_DP = 4
N_SEQ = 16
N_TENSOR = 2


def one_slab(row_key):
    cut_key = jax.random.fold_in(row_key, 0)
    spot_key = jax.random.fold_in(row_key, 2)
    longest = SLAB // 2
    remain = SLAB - longest
    index = jnp.arange(1, SLAB, dtype=jnp.int32)
    noise = jax.random.randint(cut_key, (SLAB - 1,), 0, 65536)
    ranking = jnp.where(index < remain, noise * SLAB + index, 1073741824 + index)
    order = jnp.argsort(ranking, stable=True)
    cuts = jnp.sort(index[order[:DOCS - 2]])
    bounds = jnp.concatenate([jnp.zeros((1,), jnp.int32), cuts.astype(jnp.int32), jnp.full((1,), remain, jnp.int32)])
    pieces = bounds[1:] - bounds[:-1]
    spot = jax.random.randint(spot_key, (), 0, DOCS)
    enumerated = jnp.arange(DOCS, dtype=jnp.int32)
    source = jnp.clip(enumerated - (enumerated > spot).astype(jnp.int32), 0, DOCS - 2)
    return jnp.where(enumerated == spot, longest, pieces[source]).astype(jnp.int32)


def document_lengths(key):
    return jax.vmap(one_slab)(jax.random.split(key, GROUPS))


def draw_doc_len(key, part):
    return document_lengths(key)


def draw_destination(key, part):
    lengths = document_lengths(key)
    expense = lengths * lengths
    load = jnp.sum(expense, axis=1).astype(jnp.int32)
    group = jnp.arange(GROUPS, dtype=jnp.int32)
    partner = jnp.bitwise_xor(group, GROUPS // 2)
    excess = jnp.maximum((load - load[partner]) // 2, 0)

    def pick(leftover_count, amount):
        fits = amount <= leftover_count
        return (leftover_count - jnp.where(fits, amount, 0), fits)

    def one_row(limit, row_expense):
        _, moved = lax.scan(pick, limit, row_expense[::-1])
        return moved[::-1]
    moved = jax.vmap(one_row)(excess, expense)
    return jnp.where(moved, partner[:, None], group[:, None]).astype(jnp.int32)


def draw_queries(key, part):
    key = jax.random.fold_in(key, 3)
    base_random_key = jax.random.fold_in(key, 0)
    base_offset = jnp.clip(jax.random.normal(base_random_key, (TOKEN_TOTAL, QUERY_HEADS * HEAD_SIZE), jnp.float32), -6.0, 6.0)
    return base_offset.astype(jnp.bfloat16)


def draw_keys(key, part):
    key = jax.random.fold_in(key, 5)
    base_random_key = jax.random.fold_in(key, 0)
    base_offset = jnp.clip(jax.random.normal(base_random_key, (TOKEN_TOTAL, KEY_VALUE_HEADS * HEAD_SIZE), jnp.float32), -6.0, 6.0)
    return base_offset.astype(jnp.bfloat16)


def block_scale(stream_key, shape, cuts, smallest, high):
    level = 1.0
    for dim, parts in cuts:
        draws = jax.random.uniform(jax.random.fold_in(jax.random.fold_in(stream_key, 6), dim), (parts,), jnp.float32, smallest / len(cuts), high / len(cuts))
        level = level * jnp.repeat(jnp.exp(draws), shape[dim] // parts).reshape((-1,) + (1,) * (len(shape) - 1 - dim))
    return level


def bell_draw(key, shape, deviation, reach, cuts=(), kind=jnp.bfloat16):
    level = block_scale(key, shape, cuts, -0.22, 0.18) if cuts else 1.0
    values = jax.random.normal(key, shape, jnp.float32) * deviation * level
    return jnp.minimum(jnp.maximum(values, -reach), reach).astype(kind)


def setup_inputs(seed: int = 0) -> dict:
    arg_keys = jax.random.split(jax.random.key(seed), 7)
    return {
        "queries": draw_queries(jax.random.fold_in(arg_keys[6], 71), 0),
        "keys": draw_keys(jax.random.fold_in(arg_keys[6], 71), 0),
        "values": bell_draw(arg_keys[2], (TOKEN_TOTAL, KEY_VALUE_HEADS * HEAD_SIZE), 1.0, 6.0, ((0, 64), (1, 2))),
        "out_weight": bell_draw(arg_keys[3], (QUERY_HEADS * HEAD_SIZE, D), (QUERY_HEADS * HEAD_SIZE) ** -0.5, 0.09375, ((0, 2), (1, 16))),
        "doc_len": draw_doc_len(jax.random.fold_in(arg_keys[6], 71), 0),
        "destination": draw_destination(jax.random.fold_in(arg_keys[6], 71), 0),
    }


NEG = -1e+30

def slab_labels(lengths, targets, grp):
    ends = jnp.cumsum(lengths).astype(jnp.int32)
    starts = (ends - lengths).astype(jnp.int32)
    place = jnp.arange(SLAB, dtype=jnp.int32)
    doc_index = lax.optimization_barrier(jnp.sum((ends[None, :] <= place[:, None]).astype(jnp.int32), axis=1)).astype(jnp.int32)
    onehot = (doc_index[:, None] == jnp.arange(DOCS, dtype=jnp.int32)[None, :]).astype(jnp.int32)
    position = (place - lax.optimization_barrier(jnp.sum(onehot * starts[None, :], axis=1))).astype(jnp.int32)
    target = lax.optimization_barrier(jnp.sum(onehot * targets[None, :], axis=1)).astype(jnp.int32)
    doc_id = (grp * DOCS + doc_index).astype(jnp.int32)
    return (doc_id, position, target)

def arrange(own, far):
    width = own.shape[1]
    joined = jnp.stack([own.reshape(N_SEQ, TOK_DEV, width), far.reshape(N_SEQ, TOK_DEV, width)], axis=1)
    return joined.reshape(SLOTS, width)

def arrange_labels(own, far):
    joined = jnp.stack([own.reshape(N_SEQ, TOK_DEV), far.reshape(N_SEQ, TOK_DEV)], axis=1)
    return joined.reshape(SLOTS)

def reference(queries, keys, values, out_weight, doc_len, destination):
    ratio_value = QUERY_HEADS // KEY_VALUE_HEADS
    scale = 1.0 / math.sqrt(HEAD_SIZE)
    rows_group = QUERY_HEADS * HEAD_SIZE // N_TENSOR

    def one_group(grp):
        far = jnp.bitwise_xor(grp, N_DP // 2).astype(jnp.int32)

        def take(array, index):
            return lax.dynamic_slice_in_dim(array, (index * SLAB).astype(jnp.int32), SLAB, 0)
        own_labels = slab_labels(lax.dynamic_index_in_dim(doc_len, grp, 0, False), lax.dynamic_index_in_dim(destination, grp, 0, False), grp)
        far_labels = slab_labels(lax.dynamic_index_in_dim(doc_len, far, 0, False), lax.dynamic_index_in_dim(destination, far, 0, False), far)
        slot_q = arrange(take(queries, grp), take(queries, far))
        slot_k = arrange(take(keys, grp), take(keys, far))
        slot_v = arrange(take(values, grp), take(values, far))
        doc_id = arrange_labels(own_labels[0], far_labels[0])
        position = arrange_labels(own_labels[1], far_labels[1])
        target = arrange_labels(own_labels[2], far_labels[2])
        active_slot_items = target == grp
        slot_doc = jnp.where(active_slot_items, doc_id, -1).astype(jnp.int32)
        visible = (slot_doc[:, None] == slot_doc[None, :]) & (position[None, :] <= position[:, None]) & (slot_doc[None, :] >= 0)
        active_indicator = active_slot_items.astype(jnp.float32)[:, None]

        def one_head(head):
            query_head = lax.dynamic_slice_in_dim(slot_q, (head * HEAD_SIZE).astype(jnp.int32), HEAD_SIZE, 1)
            kv_index = (head // ratio_value).astype(jnp.int32)
            key_head = lax.dynamic_slice_in_dim(slot_k, kv_index * HEAD_SIZE, HEAD_SIZE, 1)
            value_head = lax.dynamic_slice_in_dim(slot_v, kv_index * HEAD_SIZE, HEAD_SIZE, 1)
            scores = jnp.dot(query_head, key_head.T, preferred_element_type=jnp.float32) * scale
            scores = jnp.where(visible, scores, NEG)
            top = lax.optimization_barrier(jnp.max(scores, axis=1, keepdims=True))
            expo = jnp.exp(scores - top)
            total = lax.optimization_barrier(jnp.sum(expo, axis=1, keepdims=True))
            weights = (expo / total).astype(jnp.bfloat16)
            blended_outputs = jnp.dot(weights, value_head, preferred_element_type=jnp.float32)
            return (blended_outputs * active_indicator).astype(jnp.bfloat16)
        heads_out = lax.map(one_head, jnp.arange(QUERY_HEADS, dtype=jnp.int32))
        heads_out = jnp.transpose(heads_out, (1, 0, 2)).reshape(SLOTS, QUERY_HEADS * HEAD_SIZE)
        summed = jnp.zeros((SLOTS, D), jnp.float32)
        for part in range(N_TENSOR):
            lower = part * rows_group
            upper = lower + rows_group
            partial_value = jnp.dot(heads_out[:, lower:upper], out_weight[lower:upper], preferred_element_type=jnp.float32)
            partial_value = lax.optimization_barrier(partial_value.astype(jnp.bfloat16))
            summed = summed + partial_value.astype(jnp.float32)
        return summed.astype(jnp.bfloat16)
    result = lax.map(one_group, jnp.arange(N_DP, dtype=jnp.int32))
    return result.reshape(N_DP * SLOTS, D)
```

```python
import math

import jax
import jax.numpy as jnp
from jax import lax
from jax.experimental import pallas as pl
from jax.experimental.pallas import tpu as pltpu
from jax.sharding import PartitionSpec as P

MESH = pl.DeviceIdType.MESH
HEAD = 128
TOK = 128
DOCS = 16
WINDOW = 9
HALF = TOK // 2
PIECE = TOK // 4
BF16 = jnp.bfloat16
F32 = jnp.float32
NEG = -1e30


def kernel(
    q_hbm, k_hbm, v_hbm, w_hbm, len_ref, dest_ref, out_hbm,
    q_ref, w_ref, kv, gathered, bias, mine, to_pair, from_pair, far, result,
    in_sems, kv_send, kv_recv, g_send, g_recv, p_send, p_recv, x_send, x_recv, out_sem,
):
    x = lax.axis_index("dp")
    s = lax.axis_index("seq")
    t = lax.axis_index("tensor")
    z = s // 4
    y = s % 4

    def at(zz, yy):
        return (x, (zz % 4) * 4 + yy % 4, t)

    pair = (x, s, 1 - t)
    across = ((x + 2) % 4, s, t)

    in_copies = [
        pltpu.make_async_copy(k_hbm, kv.at[WINDOW - 1, :, pl.ds(0, 256)], in_sems.at[0]),
        pltpu.make_async_copy(v_hbm, kv.at[WINDOW - 1, :, pl.ds(256, 256)], in_sems.at[1]),
        pltpu.make_async_copy(q_hbm, q_ref, in_sems.at[2]),
        pltpu.make_async_copy(w_hbm, w_ref, in_sems.at[3]),
    ]
    for copy in in_copies:
        copy.start()

    barrier = pltpu.get_barrier_semaphore()
    others = [at(z, y + 1), at(z, y + 2), at(z, y + 3), at(z + 1, y), at(z + 2, y), at(z + 3, y), pair, across]
    for other in others:
        pl.semaphore_signal(barrier, inc=1, device_id=other, device_id_type=MESH)
    pl.semaphore_wait(barrier, len(others))

    def kv_copy(src, dst, index, device):
        return pltpu.make_async_remote_copy(
            src_ref=kv.at[src], dst_ref=kv.at[dst], send_sem=kv_send.at[index], recv_sem=kv_recv.at[dst],
            device_id=device, device_id_type=MESH,
        )

    def kv_wait(slot):
        pltpu.make_async_remote_copy(
            src_ref=kv.at[slot], dst_ref=kv.at[slot], send_sem=kv_send.at[0], recv_sem=kv_recv.at[slot],
            device_id=pair, device_id_type=MESH,
        ).wait_recv()

    in_copies[0].wait()
    in_copies[1].wait()
    sends = []

    def kv_start(cond, src, dst, device):
        copy = kv_copy(src, dst, len(sends), device)
        sends.append((cond, copy))

        @pl.when(cond)
        def _():
            copy.start()

    kv_start(z < 3, 8, 4, at(z + 1, y))
    kv_start(z < 2, 8, 0, at(z + 2, y))
    for step in (1, 3, 2):
        yy = (y + step) % 4
        kv_start(yy > y, 8, 8 - jnp.maximum(yy - y, 0), at(z, yy))

    @pl.when(z >= 1)
    def _():
        kv_wait(4)

    for step in (1, 3, 2):
        yy = (y + step) % 4
        kv_start(z >= 1, 4, 4 - (yy - y), at(z, yy))

    @pl.when(z >= 2)
    def _():
        kv_wait(0)

    for step in (1, 3, 2):
        yy = (y + step) % 4
        kv_start((z >= 2) & (yy < y), 0, jnp.maximum(y - yy, 0), at(z, yy))

    for half in range(2):
        q_pos = s * TOK + half * HALF + lax.broadcasted_iota(jnp.int32, (HALF, 1), 0)
        start = jnp.zeros((HALF, 1), jnp.int32)
        edge = jnp.int32(0)
        for j in range(DOCS):
            start = jnp.where(q_pos >= edge, edge, start)
            edge = edge + len_ref[0, j]
        k_pos = (s - 8) * TOK + lax.broadcasted_iota(jnp.int32, (HALF, WINDOW * TOK), 1)
        seen = (k_pos <= q_pos) & (k_pos >= start)
        bias[pl.ds(half * HALF, HALF), :] = jnp.where(seen, 0.0, NEG).astype(F32)

    for slot in (1, 2, 3, 5, 6, 7):

        @pl.when(s - 8 + slot >= 0)
        def _():
            kv_wait(slot)

    for slot in range(WINDOW - 1):

        @pl.when(s - 8 + slot < 0)
        def _():
            kv[slot] = jnp.zeros((TOK, 512), BF16)

    in_copies[2].wait()

    factor = math.log2(math.e) / math.sqrt(HEAD)

    def attend(half):
        rows = pl.ds(half * HALF, HALF)
        for j in range(2):
            key = kv[:, :, j * HEAD : (j + 1) * HEAD].reshape(WINDOW * TOK, HEAD)
            value = kv[:, :, 256 + j * HEAD : 256 + (j + 1) * HEAD].reshape(WINDOW * TOK, HEAD)
            heads = [j * 8 + h for h in range(8)]
            query = jnp.concatenate([q_ref[rows, h * HEAD : (h + 1) * HEAD] for h in heads], axis=0)
            scores = lax.dot_general(query, key, (((1,), (1,)), ((), ())), preferred_element_type=F32)
            scores = (scores.reshape(8, HALF, WINDOW * TOK) + bias[rows, :][None]).reshape(8 * HALF, WINDOW * TOK)
            top = jnp.max(scores, axis=1, keepdims=True)
            expo = jnp.exp2((scores - top) * factor)
            total = jnp.sum(expo, axis=1, keepdims=True)
            blended = jnp.dot(expo.astype(BF16), value, preferred_element_type=F32) / total
            for i, h in enumerate(heads):
                gathered[s, rows, h * HEAD : (h + 1) * HEAD] = blended[i * HALF : (i + 1) * HALF].astype(BF16)

    def block(half, first, second):
        if half == 0:
            return ((z + first) % 4) * 4 + (y + second) % 4
        return ((z + second) % 4) * 4 + (y + first) % 4

    OFFSETS = (0, 0, 1, 3, 2)

    def ring_block(half, ring, offset):
        if ring == 0:
            return block(half, offset, 0)
        return block(half, OFFSETS[ring], offset)

    def neighbour(half, ring, offset):
        along_z = (half == 0) == (ring == 0)
        return at(z + offset, y) if along_z else at(z, y + offset)

    MOVES = ((0, 0, 1), (1, 0, 3), (1, 0, 1), (0, 0, 3), (0, 3, 1), (1, 1, 3))

    def ring_ref(half, ring, offset, piece):
        return gathered.at[ring_block(half, ring, offset), pl.ds(half * HALF + piece * PIECE, PIECE)]

    def ring_copy(half, ring, i):
        piece, origin, way = MOVES[i]
        ref = ring_ref(half, ring, origin, piece)
        return pltpu.make_async_remote_copy(
            src_ref=ref, dst_ref=ref, send_sem=g_send.at[half, ring, i], recv_sem=g_recv.at[half, ring, i],
            device_id=neighbour(half, ring, way), device_id_type=MESH,
        )

    def ring_start(half, ring, moves=(0, 1, 2, 3)):
        for i in moves:
            ring_copy(half, ring, i).start()

    def ring_wait(half, ring, moves):
        for i in moves:
            piece, origin, way = MOVES[i]
            ref = ring_ref(half, ring, (origin - way) % 4, piece)
            pltpu.make_async_remote_copy(
                src_ref=ref, dst_ref=ref, send_sem=g_send.at[half, ring, i], recv_sem=g_recv.at[half, ring, i],
                device_id=pair, device_id_type=MESH,
            ).wait_recv()

    def ring_forward(half, ring):
        for i in (0, 1):
            ring_wait(half, ring, (i,))
            ring_copy(half, ring, i + 4).start()

    def pair_copy(half, b):
        ref = (b % 8, pl.ds(half * HALF, HALF))
        return pltpu.make_async_remote_copy(
            src_ref=to_pair.at[ref], dst_ref=from_pair.at[ref],
            send_sem=p_send.at[half, b % 8], recv_sem=p_recv.at[half, b % 8],
            device_id=pair, device_id_type=MESH,
        )

    def far_copy(half, c):
        rows = pl.ds(half * HALF, HALF)
        return pltpu.make_async_remote_copy(
            src_ref=far.at[c, rows], dst_ref=result.at[2 * c + 1, rows],
            send_sem=x_send.at[half, c], recv_sem=x_recv.at[half, c],
            device_id=across, device_id_type=MESH,
        )

    waiting = []

    def combine(half, b):
        @pl.when(b // 8 == t)
        def _():
            c = b % 8
            rows = pl.ds(half * HALF, HALF)
            pair_copy(half, b).wait_recv()
            total = mine[c, rows] + from_pair[c, rows].astype(F32)
            pos = b * TOK + half * HALF + lax.broadcasted_iota(jnp.int32, (HALF, 1), 0)
            goal = jnp.zeros((HALF, 1), jnp.int32)
            edge = jnp.int32(0)
            for j in range(DOCS):
                goal = jnp.where(pos >= edge, dest_ref[0, j], goal)
                edge = edge + len_ref[0, j]
            result[2 * c, rows] = jnp.where(goal == x, total, 0.0).astype(BF16)
            far[c, rows] = jnp.where(goal == x, 0.0, total).astype(BF16)
            far_copy(half, c).start()

    def project(half, ring, offsets):
        blocks = [ring_block(half, ring, o) for o in offsets]
        rows = pl.ds(half * HALF, HALF)
        left = jnp.concatenate([gathered[b, rows] for b in blocks], axis=0)
        partial = jnp.dot(left, w_ref[...], preferred_element_type=F32)
        for i, b in enumerate(blocks):
            part = partial[i * HALF : (i + 1) * HALF]

            @pl.when(b // 8 == t)
            def _():
                mine[b % 8, rows] = part

            @pl.when(b // 8 != t)
            def _():
                to_pair[b % 8, rows] = part.astype(BF16)
                pair_copy(half, b).start()

        while waiting:
            combine(*waiting.pop())
        for b in blocks:
            waiting.append((half, b))

    for half in range(2):
        attend(half)
        ring_start(half, 0)
        ring_start(half, 1)
    for half in range(2):
        ring_forward(half, 0)
        ring_forward(half, 1)
    in_copies[3].wait()
    for half in range(2):
        ring_wait(half, 0, (2, 3))
        ring_start(half, 2)
        ring_start(half, 3)
        ring_wait(half, 1, (2, 3))
        project(half, 1, (1, 3))
    for half in range(2):
        ring_wait(half, 0, (4, 5))
        ring_start(half, 4)
        ring_wait(half, 1, (4, 5))
        project(half, 1, (0, 2))
    for ring in (2, 3, 4):
        for half in range(2):
            ring_forward(half, ring)
            ring_wait(half, ring, (2, 3))
            project(half, ring, (1, 3))
        for half in range(2):
            ring_wait(half, ring, (4, 5))
            project(half, ring, (0, 2))
    while waiting:
        combine(*waiting.pop())

    for half in range(2):
        for c in range(8):
            far_copy(half, c).wait_recv()
    out = pltpu.make_async_copy(result, out_hbm, out_sem)
    out.start()
    for cond, copy in sends:

        @pl.when(cond)
        def _():
            copy.wait_send()

    for half in range(2):
        for ring in range(5):
            for i in range(6):
                ring_copy(half, ring, i).wait_send()
        for c in range(8):
            far_copy(half, c).wait_send()
            pair_copy(half, c).wait_send()
    out.wait()


def shards(queries, keys, values, out_weight, doc_len, destination):
    dma = pltpu.SemaphoreType.DMA
    hbm = pl.BlockSpec(memory_space=pl.ANY)
    smem = pl.BlockSpec(memory_space=pltpu.SMEM)
    width = out_weight.shape[1]
    out = pl.pallas_call(
        kernel,
        out_shape=jax.ShapeDtypeStruct((16, TOK, width), BF16),
        in_specs=[hbm, hbm, hbm, hbm, smem, smem],
        out_specs=hbm,
        scratch_shapes=[
            pltpu.VMEM(queries.shape, BF16),
            pltpu.VMEM(out_weight.shape, BF16),
            pltpu.VMEM((WINDOW, TOK, 512), BF16),
            pltpu.VMEM((16, TOK, queries.shape[1]), BF16),
            pltpu.VMEM((TOK, WINDOW * TOK), F32),
            pltpu.VMEM((8, TOK, width), F32),
            pltpu.VMEM((8, TOK, width), BF16),
            pltpu.VMEM((8, TOK, width), BF16),
            pltpu.VMEM((8, TOK, width), BF16),
            pltpu.VMEM((16, TOK, width), BF16),
            dma((4,)),
            dma((11,)),
            dma((WINDOW,)),
            dma((2, 5, 6)),
            dma((2, 5, 6)),
            dma((2, 8)),
            dma((2, 8)),
            dma((2, 8)),
            dma((2, 8)),
            dma(()),
        ],
        compiler_params=pltpu.CompilerParams(
            collective_id=0, has_side_effects=True, vmem_limit_bytes=56 * 2**20
        ),
        cost_estimate=pl.CostEstimate(flops=6 * 10**9, bytes_accessed=6 * 2**20, transcendentals=3 * 10**6),
    )(queries, keys, values, out_weight, doc_len, destination)
    return out.reshape(16 * TOK, width)


def solution(mesh):
    in_specs = (
        P(("dp", "seq"), "tensor"),
        P(("dp", "seq"), "tensor"),
        P(("dp", "seq"), "tensor"),
        P("tensor", "seq"),
        P("dp", None),
        P("dp", None),
    )
    out_specs = P(("dp", "tensor"), "seq")
    return jax.shard_map(shards, mesh=mesh, in_specs=in_specs, out_specs=out_specs, check_vma=False)
```

```python
import math

import jax
import jax.numpy as jnp
from jax import lax
from jax.experimental import pallas as pl
from jax.experimental.pallas import tpu as pltpu
from jax.sharding import PartitionSpec as P

MESH = pl.DeviceIdType.MESH
HEAD = 128
TOK = 128
DOCS = 16
WINDOW = 9
HALF = TOK // 2
PIECE = TOK // 4
BF16 = jnp.bfloat16
F32 = jnp.float32
NEG = -1e30


def kernel(
    q_hbm, k_hbm, v_hbm, w_hbm, len_ref, dest_ref, result,
    q_ref, w_ref, kv, gathered, bias, mine, to_pair, from_pair, near, far,
    in_sems, kv_send, kv_recv, wz_send, wz_recv, wx_send, wx_recv, z_send, z_recv, y_send, y_recv,
    p_send, p_recv, n_send, n_recv, f_send, f_recv,
):
    x = lax.axis_index("dp")
    s = lax.axis_index("seq")
    t = lax.axis_index("tensor")
    z = s // 4
    y = s % 4
    side = z // 2
    inner = z % 2
    stays = t == side
    keep = jnp.where(stays, 0, 1)
    s_other = (s + 8) % 16
    s_to = jnp.where(stays, s, s_other)
    t_to = jnp.where(stays, t, 1 - t)

    def at(zz, yy):
        return (x, (zz % 4) * 4 + yy % 4, t)

    pair = (x, s, 1 - t)
    near_to = (x, s_to, t_to)
    far_to = ((x + 2) % 4, s_to, t_to)

    in_copies = [
        pltpu.make_async_copy(k_hbm, kv.at[WINDOW - 1, :, pl.ds(0, 256)], in_sems.at[0]),
        pltpu.make_async_copy(v_hbm, kv.at[WINDOW - 1, :, pl.ds(256, 256)], in_sems.at[1]),
        pltpu.make_async_copy(q_hbm, q_ref, in_sems.at[2]),
        pltpu.make_async_copy(w_hbm, w_ref.at[0], in_sems.at[3]),
    ]
    for copy in in_copies:
        copy.start()

    barrier = pltpu.get_barrier_semaphore()
    others = [at(z, y + 1), at(z, y + 2), at(z, y + 3), at(z + 1, y), at(z + 2, y), at(z + 3, y), pair]
    others += [((x + 1) % 4, s, t), ((x + 2) % 4, s, t), ((x + 3) % 4, s, t)]
    others += [(x, s_other, 1 - t), ((x + 2) % 4, s_other, 1 - t)]
    for other in others:
        pl.semaphore_signal(barrier, inc=1, device_id=other, device_id_type=MESH)
    pl.semaphore_wait(barrier, len(others))

    def kv_copy(src, dst, index, device):
        return pltpu.make_async_remote_copy(
            src_ref=kv.at[src], dst_ref=kv.at[dst], send_sem=kv_send.at[index], recv_sem=kv_recv.at[dst],
            device_id=device, device_id_type=MESH,
        )

    def kv_wait(slot):
        pltpu.make_async_remote_copy(
            src_ref=kv.at[slot], dst_ref=kv.at[slot], send_sem=kv_send.at[0], recv_sem=kv_recv.at[slot],
            device_id=pair, device_id_type=MESH,
        ).wait_recv()

    in_copies[0].wait()
    in_copies[1].wait()
    sends = []

    def kv_start(cond, src, dst, device):
        copy = kv_copy(src, dst, len(sends), device)
        sends.append((cond, copy))

        @pl.when(cond)
        def _():
            copy.start()

    kv_start(z < 3, 8, 4, at(z + 1, y))
    kv_start(z < 2, 8, 0, at(z + 2, y))
    for step in (1, 3, 2):
        yy = (y + step) % 4
        kv_start(yy > y, 8, 8 - jnp.maximum(yy - y, 0), at(z, yy))

    def w_rows(offset, part):
        return pl.ds((x + offset) % 4 * 512 + part * 128, 128)

    def wz_copy(part):
        return pltpu.make_async_remote_copy(
            src_ref=w_hbm.at[w_rows(0, part)], dst_ref=w_ref.at[1, w_rows(0, part)],
            send_sem=wz_send.at[part], recv_sem=wz_recv.at[part],
            device_id=at(z + 2, y), device_id_type=MESH,
        )

    def wx_copy(kind, part):
        origin = 0 if kind < 2 else (3 if part % 2 == 0 else 1)
        way = (1, 3, 1 if part % 2 == 0 else 3)[kind]
        ref = w_ref.at[1, w_rows(origin, part)]
        return pltpu.make_async_remote_copy(
            src_ref=ref, dst_ref=ref, send_sem=wx_send.at[kind, part], recv_sem=wx_recv.at[kind, part],
            device_id=((x + way) % 4, s, t), device_id_type=MESH,
        )

    def wx_wait(kind, part):
        offset = (3, 1, 2)[kind]
        ref = w_ref.at[1, w_rows(offset, part)]
        pltpu.make_async_remote_copy(
            src_ref=ref, dst_ref=ref, send_sem=wx_send.at[kind, part], recv_sem=wx_recv.at[kind, part],
            device_id=pair, device_id_type=MESH,
        ).wait_recv()

    def w_spread(part):
        wz_copy(part).wait_recv()
        wx_copy(0, part).start()
        wx_copy(1, part).start()

    def w_pass(part):
        wx_wait(part % 2, part)
        wx_copy(2, part).start()

    for part in range(4):
        wz_copy(part).start()

    @pl.when(z >= 1)
    def _():
        kv_wait(4)

    for step in (1, 3, 2):
        yy = (y + step) % 4
        kv_start(z >= 1, 4, 4 - (yy - y), at(z, yy))

    @pl.when(z >= 2)
    def _():
        kv_wait(0)

    for step in (1, 3, 2):
        yy = (y + step) % 4
        kv_start((z >= 2) & (yy < y), 0, jnp.maximum(y - yy, 0), at(z, yy))

    w_spread(0)
    w_spread(1)

    for half in range(2):
        q_pos = s * TOK + half * HALF + lax.broadcasted_iota(jnp.int32, (HALF, 1), 0)
        start = jnp.zeros((HALF, 1), jnp.int32)
        edge = jnp.int32(0)
        for j in range(DOCS):
            start = jnp.where(q_pos >= edge, edge, start)
            edge = edge + len_ref[0, j]
        k_pos = (s - 8) * TOK + lax.broadcasted_iota(jnp.int32, (HALF, WINDOW * TOK), 1)
        seen = (k_pos <= q_pos) & (k_pos >= start)
        bias[pl.ds(half * HALF, HALF), :] = jnp.where(seen, 0.0, NEG).astype(F32)

    for slot in (1, 2, 3, 5, 6, 7):

        @pl.when(s - 8 + slot >= 0)
        def _():
            kv_wait(slot)

    for slot in range(WINDOW - 1):

        @pl.when(s - 8 + slot < 0)
        def _():
            kv[slot] = jnp.zeros((TOK, 512), BF16)

    w_spread(2)
    in_copies[2].wait()

    own = inner * 4 + y
    factor = math.log2(math.e) / math.sqrt(HEAD)

    def attend(half):
        rows = pl.ds(half * HALF, HALF)
        for j in range(2):
            key = kv[:, :, j * HEAD : (j + 1) * HEAD].reshape(WINDOW * TOK, HEAD)
            value = kv[:, :, 256 + j * HEAD : 256 + (j + 1) * HEAD].reshape(WINDOW * TOK, HEAD)
            heads = [j * 8 + h for h in range(8)]
            query = jnp.concatenate([q_ref[rows, h * HEAD : (h + 1) * HEAD] for h in heads], axis=0)
            scores = lax.dot_general(query, key, (((1,), (1,)), ((), ())), preferred_element_type=F32)
            scores = (scores.reshape(8, HALF, WINDOW * TOK) + bias[rows, :][None]).reshape(8 * HALF, WINDOW * TOK)
            top = jnp.max(scores, axis=1, keepdims=True)
            expo = jnp.exp2((scores - top) * factor)
            total = jnp.sum(expo, axis=1, keepdims=True)
            blended = jnp.dot(expo.astype(BF16), value, preferred_element_type=F32) / total
            for i, h in enumerate(heads):
                gathered[own, rows, h * HEAD : (h + 1) * HEAD] = blended[i * HALF : (i + 1) * HALF].astype(BF16)

    def place(o, step):
        return (inner + o) % 2 * 4 + (y + step) % 4

    def piece_ref(o, step, piece):
        return gathered.at[place(o, step), pl.ds(piece * PIECE, PIECE)]

    def z_copy(piece):
        ref = piece_ref(0, 0, piece)
        return pltpu.make_async_remote_copy(
            src_ref=ref, dst_ref=ref, send_sem=z_send.at[piece], recv_sem=z_recv.at[piece],
            device_id=at(side * 2 + 1 - inner, y), device_id_type=MESH,
        )

    def y_copy(kind, o, piece):
        origin = 0 if kind < 2 else (3 if piece % 2 == 0 else 1)
        way = (1, 3, 1 if piece % 2 == 0 else 3)[kind]
        ref = piece_ref(o, origin, piece)
        return pltpu.make_async_remote_copy(
            src_ref=ref, dst_ref=ref, send_sem=y_send.at[kind, o, piece], recv_sem=y_recv.at[kind, o, piece],
            device_id=at(z, y + way), device_id_type=MESH,
        )

    arrived = set()

    def need(o, step, piece):
        if (o, step) == (0, 0) or (o, step, piece) in arrived:
            return
        arrived.add((o, step, piece))
        ref = piece_ref(o, step, piece)
        if step == 0:
            send, recv = z_send.at[piece], z_recv.at[piece]
        else:
            kind = {3: 0, 1: 1, 2: 2}[step]
            send, recv = y_send.at[kind, o, piece], y_recv.at[kind, o, piece]
        pltpu.make_async_remote_copy(
            src_ref=ref, dst_ref=ref, send_sem=send, recv_sem=recv, device_id=pair, device_id_type=MESH
        ).wait_recv()

    def y_start(o, *pieces):
        for a, b in pieces:
            need(o, 0, a)
            need(o, 0, b)
            y_copy(0, o, a).start()
            y_copy(1, o, b).start()

    def y_pass(o, *pieces):
        for piece in pieces:
            need(o, 3 if piece % 2 == 0 else 1, piece)
            y_copy(2, o, piece).start()

    def pair_copy(half, c):
        ref = (c, pl.ds(half * HALF, HALF))
        return pltpu.make_async_remote_copy(
            src_ref=to_pair.at[ref], dst_ref=from_pair.at[ref],
            send_sem=p_send.at[half, c], recv_sem=p_recv.at[half, c],
            device_id=pair, device_id_type=MESH,
        )

    def near_copy(half, c):
        rows = pl.ds(half * HALF, HALF)
        return pltpu.make_async_remote_copy(
            src_ref=near.at[c, rows], dst_ref=result.at[2 * c, rows],
            send_sem=n_send.at[half, c], recv_sem=n_recv.at[half, c],
            device_id=near_to, device_id_type=MESH,
        )

    def far_copy(half, c):
        rows = pl.ds(half * HALF, HALF)
        return pltpu.make_async_remote_copy(
            src_ref=far.at[c, rows], dst_ref=result.at[2 * c + 1, rows],
            send_sem=f_send.at[half, c], recv_sem=f_recv.at[half, c],
            device_id=far_to, device_id_type=MESH,
        )

    waiting = []

    def combine(half, c):
        rows = pl.ds(half * HALF, HALF)
        pair_copy(half, c).wait_recv()
        total = mine[c, rows] + from_pair[c, rows].astype(F32)
        pos = (side * 8 + c) * TOK + half * HALF + lax.broadcasted_iota(jnp.int32, (HALF, 1), 0)
        goal = jnp.zeros((HALF, 1), jnp.int32)
        edge = jnp.int32(0)
        for j in range(DOCS):
            goal = jnp.where(pos >= edge, dest_ref[0, j], goal)
            edge = edge + len_ref[0, j]
        far[c, rows] = jnp.where(goal == x, 0.0, total).astype(BF16)
        far_copy(half, c).start()
        kept = jnp.where(goal == x, total, 0.0).astype(BF16)

        @pl.when(stays)
        def _():
            result[2 * c, rows] = kept

        @pl.when(jnp.logical_not(stays))
        def _():
            near[c, rows] = kept
            near_copy(half, c).start()

    def project(*parts):
        for o, step, half in parts:
            for piece in (2 * half, 2 * half + 1):
                need(o, step, piece)
        places = [(place(o, step), pl.ds(half * HALF, HALF)) for o, step, half in parts]
        left = [gathered[c, rows] for c, rows in places]
        left = left[0] if len(left) == 1 else jnp.concatenate(left, axis=0)
        given = jnp.dot(left, w_ref[1 - keep], preferred_element_type=F32)
        for i, ((c, rows), (_, _, half)) in enumerate(zip(places, parts)):
            to_pair[c, rows] = given[i * HALF : (i + 1) * HALF].astype(BF16)
            pair_copy(half, c).start()
        kept = jnp.dot(left, w_ref[keep], preferred_element_type=F32)
        for i, (c, rows) in enumerate(places):
            mine[c, rows] = kept[i * HALF : (i + 1) * HALF]
        while waiting:
            combine(*waiting.pop(0))
        for (c, _), (_, _, half) in zip(places, parts):
            waiting.append((half, c))

    attend(0)
    z_copy(0).start()
    z_copy(1).start()
    y_start(0, (0, 1), (1, 0))
    w_spread(3)
    w_pass(0)
    attend(1)
    z_copy(2).start()
    z_copy(3).start()
    y_start(0, (2, 3), (3, 2))
    w_pass(1)
    w_pass(2)
    y_start(1, (0, 1))
    y_pass(0, 0, 1)
    y_start(1, (1, 0))
    w_pass(3)
    y_start(1, (2, 3))
    in_copies[3].wait()
    for part in range(4):
        wx_wait(1 - part % 2, part)
        wx_wait(2, part)
    project((0, 0, 0), (0, 0, 1))
    y_pass(1, 0, 1)
    y_start(1, (3, 2))
    project((0, 1, 0), (0, 3, 0))
    y_pass(0, 2, 3)
    project((1, 0, 0), (1, 0, 1))
    y_pass(1, 2, 3)
    project((0, 1, 1), (0, 3, 1))
    project((1, 1, 0), (1, 3, 0))
    project((0, 2, 0), (1, 2, 0))
    project((1, 1, 1), (1, 3, 1))
    project((0, 2, 1))
    project((1, 2, 1))
    while waiting:
        combine(*waiting.pop(0))

    for half in range(2):
        for c in range(8):
            far_copy(half, c).wait()
            pair_copy(half, c).wait_send()

            @pl.when(jnp.logical_not(stays))
            def _():
                near_copy(half, c).wait()

    for cond, copy in sends:

        @pl.when(cond)
        def _():
            copy.wait_send()

    for part in range(4):
        wz_copy(part).wait_send()
        z_copy(part).wait_send()
        for kind in range(3):
            wx_copy(kind, part).wait_send()
            for o in range(2):
                y_copy(kind, o, part).wait_send()


def shards(queries, keys, values, out_weight, doc_len, destination):
    dma = pltpu.SemaphoreType.DMA
    hbm = pl.BlockSpec(memory_space=pl.ANY)
    smem = pl.BlockSpec(memory_space=pltpu.SMEM)
    width = out_weight.shape[1]
    out = pl.pallas_call(
        kernel,
        out_shape=pltpu.VMEM((16, TOK, width), BF16),
        in_specs=[hbm, hbm, hbm, hbm, smem, smem],
        out_specs=pl.BlockSpec(memory_space=pltpu.VMEM),
        scratch_shapes=[
            pltpu.VMEM(queries.shape, BF16),
            pltpu.VMEM((2,) + out_weight.shape, BF16),
            pltpu.VMEM((WINDOW, TOK, 512), BF16),
            pltpu.VMEM((8, TOK, queries.shape[1]), BF16),
            pltpu.VMEM((TOK, WINDOW * TOK), F32),
            pltpu.VMEM((8, TOK, width), F32),
            pltpu.VMEM((8, TOK, width), BF16),
            pltpu.VMEM((8, TOK, width), BF16),
            pltpu.VMEM((8, TOK, width), BF16),
            pltpu.VMEM((8, TOK, width), BF16),
            dma((4,)),
            dma((11,)),
            dma((WINDOW,)),
            dma((4,)),
            dma((4,)),
            dma((3, 4)),
            dma((3, 4)),
            dma((4,)),
            dma((4,)),
            dma((3, 2, 4)),
            dma((3, 2, 4)),
            dma((2, 8)),
            dma((2, 8)),
            dma((2, 8)),
            dma((2, 8)),
            dma((2, 8)),
            dma((2, 8)),
        ],
        compiler_params=pltpu.CompilerParams(
            collective_id=0, has_side_effects=True, vmem_limit_bytes=56 * 2**20
        ),
        cost_estimate=pl.CostEstimate(flops=6 * 10**9, bytes_accessed=6 * 2**20, transcendentals=3 * 10**6),
    )(queries, keys, values, out_weight, doc_len, destination)
    return out.reshape(16 * TOK, width)


def solution(mesh):
    in_specs = (
        P(("dp", "seq"), "tensor"),
        P(("dp", "seq"), "tensor"),
        P(("dp", "seq"), "tensor"),
        P("tensor", "seq"),
        P("dp", None),
        P("dp", None),
    )
    out_specs = P(("dp", "tensor"), "seq")
    return jax.shard_map(shards, mesh=mesh, in_specs=in_specs, out_specs=out_specs, check_vma=False)
```

```python
import math

import jax
import jax.numpy as jnp
from jax import lax
from jax.experimental import pallas as pl
from jax.experimental.pallas import tpu as pltpu
from jax.sharding import PartitionSpec as P

MESH = pl.DeviceIdType.MESH
HEAD = 128
TOK = 128
DOCS = 16
WINDOW = 9
HALF = TOK // 2
BF16 = jnp.bfloat16
F32 = jnp.float32
NEG = -1e30


def kernel(
    q_hbm, k_hbm, v_hbm, w_hbm, len_ref, dest_ref, result,
    q_ref, w_ref, kv, gathered, bias, mine, to_pair, from_pair, near, far,
    in_sems, kv_send, kv_recv, wz_send, wz_recv, wx_send, wx_recv, z_send, z_recv, y_send, y_recv,
    p_send, p_recv, n_send, n_recv, f_send, f_recv,
):
    x = lax.axis_index("dp")
    s = lax.axis_index("seq")
    t = lax.axis_index("tensor")
    z = s // 4
    y = s % 4
    side = z // 2
    inner = z % 2
    stays = t == side
    keep = jnp.where(stays, 0, 1)
    s_other = (s + 8) % 16
    s_to = jnp.where(stays, s, s_other)
    t_to = jnp.where(stays, t, 1 - t)

    def at(zz, yy):
        return (x, (zz % 4) * 4 + yy % 4, t)

    pair = (x, s, 1 - t)
    near_to = (x, s_to, t_to)
    far_to = ((x + 2) % 4, s_to, t_to)

    in_copies = [
        pltpu.make_async_copy(
            ref.at[:, pl.ds(j * HEAD, HEAD)], kv.at[WINDOW - 1, j, :, pl.ds(n * HEAD, HEAD)], in_sems.at[2 * j + n]
        )
        for j in range(2)
        for n, ref in enumerate((k_hbm, v_hbm))
    ]
    in_copies += [
        pltpu.make_async_copy(q_hbm, q_ref, in_sems.at[4]),
        pltpu.make_async_copy(w_hbm, w_ref.at[0], in_sems.at[5]),
    ]
    for copy in in_copies:
        copy.start()

    barrier = pltpu.get_barrier_semaphore()
    others = [at(z, y + 1), at(z, y + 2), at(z, y + 3), at(z + 1, y), at(z + 2, y), at(z + 3, y), pair]
    others += [((x + 1) % 4, s, t), ((x + 2) % 4, s, t), ((x + 3) % 4, s, t)]
    others += [(x, s_other, 1 - t), ((x + 2) % 4, s_other, 1 - t)]
    for other in others:
        pl.semaphore_signal(barrier, inc=1, device_id=other, device_id_type=MESH)
    pl.semaphore_wait(barrier, len(others))

    def kv_copy(head, src, dst, index, device):
        return pltpu.make_async_remote_copy(
            src_ref=kv.at[src, head], dst_ref=kv.at[dst, head],
            send_sem=kv_send.at[head, index], recv_sem=kv_recv.at[head, dst],
            device_id=device, device_id_type=MESH,
        )

    def kv_wait(head, slot):
        @pl.when(s - 8 + slot >= 0)
        def _():
            pltpu.make_async_remote_copy(
                src_ref=kv.at[slot, head], dst_ref=kv.at[slot, head],
                send_sem=kv_send.at[head, 0], recv_sem=kv_recv.at[head, slot],
                device_id=pair, device_id_type=MESH,
            ).wait_recv()

    sends = []

    def kv_start(head, index, cond, src, dst, device):
        copy = kv_copy(head, src, dst, index, device)
        sends.append((cond, copy))

        @pl.when(cond)
        def _():
            copy.start()

    steps = [(n, (y + step) % 4) for n, step in enumerate((1, 3, 2))]

    def kv_column(head):
        in_copies[2 * head].wait()
        in_copies[2 * head + 1].wait()
        kv_start(head, 0, z < 3, 8, 4, at(z + 1, y))
        kv_start(head, 1, z < 2, 8, 0, at(z + 2, y))

    def kv_row(head):
        for n, yy in steps:
            kv_start(head, 2 + n, yy > y, 8, 8 - jnp.maximum(yy - y, 0), at(z, yy))

    def kv_relay(head):
        kv_wait(head, 4)
        for n, yy in steps:
            kv_start(head, 5 + n, z >= 1, 4, 4 - (yy - y), at(z, yy))
        kv_wait(head, 0)
        for n, yy in steps:
            kv_start(head, 8 + n, (z >= 2) & (yy < y), 0, jnp.maximum(y - yy, 0), at(z, yy))

    def kv_rest(head):
        for slot in (5, 6, 7, 1, 2, 3):
            kv_wait(head, slot)
        for slot in range(WINDOW - 1):

            @pl.when(s - 8 + slot < 0)
            def _():
                kv[slot, head] = jnp.zeros((TOK, 2 * HEAD), BF16)

    def w_rows(offset, part):
        return pl.ds((x + offset) % 4 * 512 + part * 128, 128)

    def wz_copy(part):
        return pltpu.make_async_remote_copy(
            src_ref=w_hbm.at[w_rows(0, part)], dst_ref=w_ref.at[1, w_rows(0, part)],
            send_sem=wz_send.at[part], recv_sem=wz_recv.at[part],
            device_id=at(z + 2, y), device_id_type=MESH,
        )

    def wx_copy(kind, part):
        origin = 0 if kind < 2 else (3 if part % 2 == 0 else 1)
        way = (1, 3, 1 if part % 2 == 0 else 3)[kind]
        ref = w_ref.at[1, w_rows(origin, part)]
        return pltpu.make_async_remote_copy(
            src_ref=ref, dst_ref=ref, send_sem=wx_send.at[kind, part], recv_sem=wx_recv.at[kind, part],
            device_id=((x + way) % 4, s, t), device_id_type=MESH,
        )

    def wx_wait(kind, part):
        offset = (3, 1, 2)[kind]
        ref = w_ref.at[1, w_rows(offset, part)]
        pltpu.make_async_remote_copy(
            src_ref=ref, dst_ref=ref, send_sem=wx_send.at[kind, part], recv_sem=wx_recv.at[kind, part],
            device_id=pair, device_id_type=MESH,
        ).wait_recv()

    def w_spread(part):
        wz_copy(part).wait_recv()
        wx_copy(0, part).start()
        wx_copy(1, part).start()

    def w_pass(part):
        wx_wait(part % 2, part)
        wx_copy(2, part).start()


    kv_column(0)
    kv_row(0)
    wz_copy(0).start()
    kv_column(1)
    for part in range(1, 4):
        wz_copy(part).start()
    kv_relay(0)
    kv_row(1)
    kv_relay(1)

    for half in range(2):
        q_pos = s * TOK + half * HALF + lax.broadcasted_iota(jnp.int32, (HALF, 1), 0)
        start = jnp.zeros((HALF, 1), jnp.int32)
        edge = jnp.int32(0)
        for j in range(DOCS):
            start = jnp.where(q_pos >= edge, edge, start)
            edge = edge + len_ref[0, j]
        k_pos = (s - 8) * TOK + lax.broadcasted_iota(jnp.int32, (HALF, WINDOW * TOK), 1)
        seen = (k_pos <= q_pos) & (k_pos >= start)
        bias[pl.ds(half * HALF, HALF), :] = jnp.where(seen, 0.0, NEG).astype(F32)

    in_copies[4].wait()

    own = inner * 4 + y
    factor = math.log2(math.e) / math.sqrt(HEAD)

    def attend(half, j):
        rows = pl.ds(half * HALF, HALF)
        key = kv[:, j, :, :HEAD].reshape(WINDOW * TOK, HEAD)
        value = kv[:, j, :, HEAD:].reshape(WINDOW * TOK, HEAD)
        query = jnp.concatenate([q_ref[rows, (j * 8 + h) * HEAD : (j * 8 + h + 1) * HEAD] for h in range(8)], axis=0)
        scores = lax.dot_general(query, key, (((1,), (1,)), ((), ())), preferred_element_type=F32)
        scores = (scores.reshape(8, HALF, WINDOW * TOK) + bias[rows, :][None]).reshape(8 * HALF, WINDOW * TOK)
        top = jnp.max(scores, axis=1, keepdims=True)
        expo = jnp.exp2((scores - top) * factor)
        total = jnp.sum(expo, axis=1, keepdims=True)
        blended = jnp.dot(expo.astype(BF16), value, preferred_element_type=F32) / total
        for h in range(8):
            gathered[own, j, rows, h * HEAD : (h + 1) * HEAD] = blended[h * HALF : (h + 1) * HALF].astype(BF16)

    def place(o, step):
        return (inner + o) % 2 * 4 + (y + step) % 4

    def piece_ref(o, step, piece):
        return gathered.at[place(o, step), piece % 2, pl.ds(piece // 2 * HALF, HALF)]

    def z_copy(piece):
        ref = piece_ref(0, 0, piece)
        return pltpu.make_async_remote_copy(
            src_ref=ref, dst_ref=ref, send_sem=z_send.at[piece], recv_sem=z_recv.at[piece],
            device_id=at(side * 2 + 1 - inner, y), device_id_type=MESH,
        )

    def y_copy(kind, o, piece):
        origin = 0 if kind < 2 else (3 if piece % 2 == 0 else 1)
        way = (1, 3, 1 if piece % 2 == 0 else 3)[kind]
        ref = piece_ref(o, origin, piece)
        return pltpu.make_async_remote_copy(
            src_ref=ref, dst_ref=ref, send_sem=y_send.at[kind, o, piece], recv_sem=y_recv.at[kind, o, piece],
            device_id=at(z, y + way), device_id_type=MESH,
        )

    arrived = set()

    def need(o, step, piece):
        if (o, step) == (0, 0) or (o, step, piece) in arrived:
            return
        arrived.add((o, step, piece))
        ref = piece_ref(o, step, piece)
        if step == 0:
            send, recv = z_send.at[piece], z_recv.at[piece]
        else:
            kind = {3: 0, 1: 1, 2: 2}[step]
            send, recv = y_send.at[kind, o, piece], y_recv.at[kind, o, piece]
        pltpu.make_async_remote_copy(
            src_ref=ref, dst_ref=ref, send_sem=send, recv_sem=recv, device_id=pair, device_id_type=MESH
        ).wait_recv()

    def y_start(o, *pieces):
        for a, b in pieces:
            need(o, 0, a)
            need(o, 0, b)
            y_copy(0, o, a).start()
            y_copy(1, o, b).start()

    def y_pass(o, *pieces):
        for piece in pieces:
            need(o, 3 if piece % 2 == 0 else 1, piece)
            y_copy(2, o, piece).start()

    def pair_copy(half, c):
        ref = (c, pl.ds(half * HALF, HALF))
        return pltpu.make_async_remote_copy(
            src_ref=to_pair.at[ref], dst_ref=from_pair.at[ref],
            send_sem=p_send.at[half, c], recv_sem=p_recv.at[half, c],
            device_id=pair, device_id_type=MESH,
        )

    def near_copy(half, c):
        rows = pl.ds(half * HALF, HALF)
        return pltpu.make_async_remote_copy(
            src_ref=near.at[c, rows], dst_ref=result.at[2 * c, rows],
            send_sem=n_send.at[half, c], recv_sem=n_recv.at[half, c],
            device_id=near_to, device_id_type=MESH,
        )

    def far_copy(half, c):
        rows = pl.ds(half * HALF, HALF)
        return pltpu.make_async_remote_copy(
            src_ref=far.at[c, rows], dst_ref=result.at[2 * c + 1, rows],
            send_sem=f_send.at[half, c], recv_sem=f_recv.at[half, c],
            device_id=far_to, device_id_type=MESH,
        )

    done = []

    def combine(half, c):
        rows = pl.ds(half * HALF, HALF)
        pair_copy(half, c).wait_recv()
        total = mine[c, rows] + from_pair[c, rows].astype(F32)
        pos = (side * 8 + c) * TOK + half * HALF + lax.broadcasted_iota(jnp.int32, (HALF, 1), 0)
        goal = jnp.zeros((HALF, 1), jnp.int32)
        edge = jnp.int32(0)
        for j in range(DOCS):
            goal = jnp.where(pos >= edge, dest_ref[0, j], goal)
            edge = edge + len_ref[0, j]
        far[c, rows] = jnp.where(goal == x, 0.0, total).astype(BF16)
        far_copy(half, c).start()
        kept = jnp.where(goal == x, total, 0.0).astype(BF16)

        @pl.when(stays)
        def _():
            result[2 * c, rows] = kept

        @pl.when(jnp.logical_not(stays))
        def _():
            near[c, rows] = kept
            near_copy(half, c).start()

    def project(*parts):
        for o, step, half in parts:
            for piece in (2 * half, 2 * half + 1):
                need(o, step, piece)
        places = [(place(o, step), pl.ds(half * HALF, HALF)) for o, step, half in parts]
        left = [jnp.concatenate([gathered[c, 0, rows], gathered[c, 1, rows]], axis=1) for c, rows in places]
        left = left[0] if len(left) == 1 else jnp.concatenate(left, axis=0)
        given = jnp.dot(left, w_ref[1 - keep], preferred_element_type=F32)
        for i, ((c, rows), (_, _, half)) in enumerate(zip(places, parts)):
            to_pair[c, rows] = given[i * HALF : (i + 1) * HALF].astype(BF16)
            pair_copy(half, c).start()
        kept = jnp.dot(left, w_ref[keep], preferred_element_type=F32)
        for i, (c, rows) in enumerate(places):
            mine[c, rows] = kept[i * HALF : (i + 1) * HALF]
        for (c, _), (_, _, half) in zip(places, parts):
            combine(half, c)
            done.append((half, c))

    def finish(half, c):
        pair_copy(half, c).wait_send()
        far_copy(half, c).wait()

        @pl.when(jnp.logical_not(stays))
        def _():
            near_copy(half, c).wait()

    w_spread(0)
    kv_rest(0)
    attend(0, 0)
    z_copy(0).start()
    y_copy(0, 0, 0).start()
    y_copy(1, 0, 0).start()
    w_spread(1)
    attend(1, 0)
    z_copy(2).start()
    kv_rest(1)
    attend(0, 1)
    z_copy(1).start()
    y_copy(0, 0, 1).start()
    y_copy(1, 0, 1).start()
    w_spread(2)
    w_pass(0)
    attend(1, 1)
    z_copy(3).start()
    w_spread(3)
    w_pass(1)
    y_start(1, (0, 1), (1, 0))
    y_pass(0, 0, 1)
    w_pass(2)
    y_start(0, (2, 3), (3, 2))
    w_pass(3)
    y_pass(1, 0, 1)
    in_copies[5].wait()
    for part in range(4):
        wx_wait(1 - part % 2, part)
        wx_wait(2, part)
    project((0, 0, 0), (0, 0, 1))
    project((0, 1, 0), (0, 3, 0))
    y_start(1, (2, 3), (3, 2))
    project((1, 0, 0), (1, 0, 1))
    y_pass(0, 2, 3)
    project((1, 1, 0), (1, 3, 0))
    project((0, 2, 0), (1, 2, 0))
    y_pass(1, 2, 3)
    project((0, 1, 1), (0, 3, 1))
    for cond, copy in sends:

        @pl.when(cond)
        def _():
            copy.wait_send()

    for part in range(4):
        wz_copy(part).wait_send()
        z_copy(part).wait_send()
        for kind in range(3):
            wx_copy(kind, part).wait_send()
            y_copy(kind, 0, part).wait_send()
    project((1, 1, 1), (1, 3, 1))
    for half, c in done[:8]:
        finish(half, c)
    project((0, 2, 1))
    project((1, 2, 1))
    for part in range(4):
        for kind in range(3):
            y_copy(kind, 1, part).wait_send()
    for half, c in done[8:]:
        finish(half, c)


def shards(queries, keys, values, out_weight, doc_len, destination):
    dma = pltpu.SemaphoreType.DMA
    hbm = pl.BlockSpec(memory_space=pl.ANY)
    smem = pl.BlockSpec(memory_space=pltpu.SMEM)
    width = out_weight.shape[1]
    out = pl.pallas_call(
        kernel,
        out_shape=pltpu.VMEM((16, TOK, width), BF16),
        in_specs=[hbm, hbm, hbm, hbm, smem, smem],
        out_specs=pl.BlockSpec(memory_space=pltpu.VMEM),
        scratch_shapes=[
            pltpu.VMEM(queries.shape, BF16),
            pltpu.VMEM((2,) + out_weight.shape, BF16),
            pltpu.VMEM((WINDOW, 2, TOK, 2 * HEAD), BF16),
            pltpu.VMEM((8, 2, TOK, queries.shape[1] // 2), BF16),
            pltpu.VMEM((TOK, WINDOW * TOK), F32),
            pltpu.VMEM((8, TOK, width), F32),
            pltpu.VMEM((8, TOK, width), BF16),
            pltpu.VMEM((8, TOK, width), BF16),
            pltpu.VMEM((8, TOK, width), BF16),
            pltpu.VMEM((8, TOK, width), BF16),
            dma((6,)),
            dma((2, 11)),
            dma((2, WINDOW)),
            dma((4,)),
            dma((4,)),
            dma((3, 4)),
            dma((3, 4)),
            dma((4,)),
            dma((4,)),
            dma((3, 2, 4)),
            dma((3, 2, 4)),
            dma((2, 8)),
            dma((2, 8)),
            dma((2, 8)),
            dma((2, 8)),
            dma((2, 8)),
            dma((2, 8)),
        ],
        compiler_params=pltpu.CompilerParams(
            collective_id=0, has_side_effects=True, vmem_limit_bytes=56 * 2**20
        ),
        cost_estimate=pl.CostEstimate(flops=6 * 10**9, bytes_accessed=6 * 2**20, transcendentals=3 * 10**6),
    )(queries, keys, values, out_weight, doc_len, destination)
    return out.reshape(16 * TOK, width)


def solution(mesh):
    in_specs = (
        P(("dp", "seq"), "tensor"),
        P(("dp", "seq"), "tensor"),
        P(("dp", "seq"), "tensor"),
        P("tensor", "seq"),
        P("dp", None),
        P("dp", None),
    )
    out_specs = P(("dp", "tensor"), "seq")
    return jax.shard_map(shards, mesh=mesh, in_specs=in_specs, out_specs=out_specs, check_vma=False)
```

```python
import math

import jax
import jax.numpy as jnp
from jax import lax
from jax.experimental import pallas as pl
from jax.experimental.pallas import tpu as pltpu
from jax.sharding import PartitionSpec as P

MESH = pl.DeviceIdType.MESH
HEAD = 128
TOK = 128
DOCS = 16
WINDOW = 9
HALF = TOK // 2
BF16 = jnp.bfloat16
F32 = jnp.float32
NEG = -1e30


def kernel(
    q_hbm, k_hbm, v_hbm, w_hbm, len_ref, dest_ref, result,
    q_ref, w_ref, kv, gathered, bias, mine, to_pair, from_pair, near, far,
    in_sems, kv_send, kv_recv, wz_send, wz_recv, wx_send, wx_recv, z_send, z_recv, y_send, y_recv,
    p_send, p_recv, n_send, n_recv, f_send, f_recv,
):
    x = lax.axis_index("dp")
    s = lax.axis_index("seq")
    t = lax.axis_index("tensor")
    z = s // 4
    y = s % 4
    side = z // 2
    inner = z % 2
    stays = t == side
    keep = jnp.where(stays, 0, 1)
    s_other = (s + 8) % 16
    s_to = jnp.where(stays, s, s_other)
    t_to = jnp.where(stays, t, 1 - t)

    def at(zz, yy):
        return (x, (zz % 4) * 4 + yy % 4, t)

    pair = (x, s, 1 - t)
    near_to = (x, s_to, t_to)
    far_to = ((x + 2) % 4, s_to, t_to)

    in_copies = [
        pltpu.make_async_copy(
            ref.at[:, pl.ds(j * HEAD, HEAD)], kv.at[WINDOW - 1, j, :, pl.ds(n * HEAD, HEAD)], in_sems.at[2 * j + n]
        )
        for j in range(2)
        for n, ref in enumerate((k_hbm, v_hbm))
    ]
    in_copies += [
        pltpu.make_async_copy(q_hbm, q_ref, in_sems.at[4]),
        pltpu.make_async_copy(w_hbm, w_ref.at[0], in_sems.at[5]),
    ]
    for copy in in_copies:
        copy.start()

    barrier = pltpu.get_barrier_semaphore()
    others = [at(z, y + 1), at(z, y + 2), at(z, y + 3), at(z + 1, y), at(z + 2, y), at(z + 3, y), pair]
    others += [((x + 1) % 4, s, t), ((x + 2) % 4, s, t), ((x + 3) % 4, s, t)]
    others += [(x, s_other, 1 - t), ((x + 2) % 4, s_other, 1 - t)]
    for other in others:
        pl.semaphore_signal(barrier, inc=1, device_id=other, device_id_type=MESH)
    pl.semaphore_wait(barrier, len(others))

    def kv_copy(head, src, dst, index, device):
        return pltpu.make_async_remote_copy(
            src_ref=kv.at[src, head], dst_ref=kv.at[dst, head],
            send_sem=kv_send.at[head, index], recv_sem=kv_recv.at[head, dst],
            device_id=device, device_id_type=MESH,
        )

    def kv_wait(head, slot):
        @pl.when(s - 8 + slot >= 0)
        def _():
            pltpu.make_async_remote_copy(
                src_ref=kv.at[slot, head], dst_ref=kv.at[slot, head],
                send_sem=kv_send.at[head, 0], recv_sem=kv_recv.at[head, slot],
                device_id=pair, device_id_type=MESH,
            ).wait_recv()

    sends = []

    def kv_start(head, index, cond, src, dst, device):
        copy = kv_copy(head, src, dst, index, device)
        sends.append((cond, copy))

        @pl.when(cond)
        def _():
            copy.start()

    steps = [(n, (y + step) % 4) for n, step in enumerate((1, 3, 2))]

    def kv_column(head):
        in_copies[2 * head].wait()
        in_copies[2 * head + 1].wait()
        kv_start(head, 0, z < 3, 8, 4, at(z + 1, y))
        kv_start(head, 1, z < 2, 8, 0, at(z + 2, y))

    def kv_row(head):
        for n, yy in steps:
            kv_start(head, 2 + n, yy > y, 8, 8 - jnp.maximum(yy - y, 0), at(z, yy))

    def kv_relay(head):
        kv_wait(head, 4)
        for n, yy in steps:
            kv_start(head, 5 + n, z >= 1, 4, 4 - (yy - y), at(z, yy))
        kv_wait(head, 0)
        for n, yy in steps:
            kv_start(head, 8 + n, (z >= 2) & (yy < y), 0, jnp.maximum(y - yy, 0), at(z, yy))

    def kv_rest(head):
        for slot in (5, 6, 7, 1, 2, 3):
            kv_wait(head, slot)
        for slot in range(WINDOW - 1):

            @pl.when(s - 8 + slot < 0)
            def _():
                kv[slot, head] = jnp.zeros((TOK, 2 * HEAD), BF16)

    def w_rows(offset, part):
        return pl.ds((x + offset) % 4 * 512 + part * 128, 128)

    def wz_copy(part):
        return pltpu.make_async_remote_copy(
            src_ref=w_hbm.at[w_rows(0, part)], dst_ref=w_ref.at[1, w_rows(0, part)],
            send_sem=wz_send.at[part], recv_sem=wz_recv.at[part],
            device_id=at(z + 2, y), device_id_type=MESH,
        )

    def wx_copy(kind, part):
        origin = 0 if kind < 2 else (3 if part % 2 == 0 else 1)
        way = (1, 3, 1 if part % 2 == 0 else 3)[kind]
        ref = w_ref.at[1, w_rows(origin, part)]
        return pltpu.make_async_remote_copy(
            src_ref=ref, dst_ref=ref, send_sem=wx_send.at[kind, part], recv_sem=wx_recv.at[kind, part],
            device_id=((x + way) % 4, s, t), device_id_type=MESH,
        )

    def wx_wait(kind, part):
        offset = (3, 1, 2)[kind]
        ref = w_ref.at[1, w_rows(offset, part)]
        pltpu.make_async_remote_copy(
            src_ref=ref, dst_ref=ref, send_sem=wx_send.at[kind, part], recv_sem=wx_recv.at[kind, part],
            device_id=pair, device_id_type=MESH,
        ).wait_recv()

    def w_spread(part):
        wz_copy(part).wait_recv()
        wx_copy(0, part).start()
        wx_copy(1, part).start()

    def w_pass(part):
        wx_wait(part % 2, part)
        wx_copy(2, part).start()


    kv_column(0)
    kv_row(0)
    wz_copy(0).start()
    kv_column(1)
    for part in range(1, 4):
        wz_copy(part).start()
    kv_relay(0)
    kv_row(1)
    kv_relay(1)

    for half in range(2):
        q_pos = s * TOK + half * HALF + lax.broadcasted_iota(jnp.int32, (HALF, 1), 0)
        start = jnp.zeros((HALF, 1), jnp.int32)
        edge = jnp.int32(0)
        for j in range(DOCS):
            start = jnp.where(q_pos >= edge, edge, start)
            edge = edge + len_ref[0, j]
        k_pos = (s - 8) * TOK + lax.broadcasted_iota(jnp.int32, (HALF, WINDOW * TOK), 1)
        seen = (k_pos <= q_pos) & (k_pos >= start)
        bias[pl.ds(half * HALF, HALF), :] = jnp.where(seen, 0.0, NEG).astype(F32)

    in_copies[4].wait()

    own = inner * 4 + y
    factor = math.log2(math.e) / math.sqrt(HEAD)

    def attend(half, j):
        rows = pl.ds(half * HALF, HALF)
        key = kv[:, j, :, :HEAD].reshape(WINDOW * TOK, HEAD)
        value = kv[:, j, :, HEAD:].reshape(WINDOW * TOK, HEAD)
        query = jnp.concatenate([q_ref[rows, (j * 8 + h) * HEAD : (j * 8 + h + 1) * HEAD] for h in range(8)], axis=0)
        scores = lax.dot_general(query, key, (((1,), (1,)), ((), ())), preferred_element_type=F32)
        scores = (scores.reshape(8, HALF, WINDOW * TOK) + bias[rows, :][None]).reshape(8 * HALF, WINDOW * TOK)
        top = jnp.max(scores, axis=1, keepdims=True)
        expo = jnp.exp2((scores - top) * factor)
        total = jnp.sum(expo, axis=1, keepdims=True)
        blended = jnp.dot(expo.astype(BF16), value, preferred_element_type=F32) / total
        for h in range(8):
            gathered[own, j, rows, h * HEAD : (h + 1) * HEAD] = blended[h * HALF : (h + 1) * HALF].astype(BF16)

    def place(o, step):
        return (inner + o) % 2 * 4 + (y + step) % 4

    def piece_ref(o, step, piece):
        return gathered.at[place(o, step), piece % 2, pl.ds(piece // 2 * HALF, HALF)]

    def z_copy(piece):
        ref = piece_ref(0, 0, piece)
        return pltpu.make_async_remote_copy(
            src_ref=ref, dst_ref=ref, send_sem=z_send.at[piece], recv_sem=z_recv.at[piece],
            device_id=at(side * 2 + 1 - inner, y), device_id_type=MESH,
        )

    def y_copy(kind, o, piece):
        origin = 0 if kind < 2 else (3 if piece % 2 == 0 else 1)
        way = (1, 3, 1 if piece % 2 == 0 else 3)[kind]
        ref = piece_ref(o, origin, piece)
        return pltpu.make_async_remote_copy(
            src_ref=ref, dst_ref=ref, send_sem=y_send.at[kind, o, piece], recv_sem=y_recv.at[kind, o, piece],
            device_id=at(z, y + way), device_id_type=MESH,
        )

    arrived = set()

    def need(o, step, piece):
        if (o, step) == (0, 0) or (o, step, piece) in arrived:
            return
        arrived.add((o, step, piece))
        ref = piece_ref(o, step, piece)
        if step == 0:
            send, recv = z_send.at[piece], z_recv.at[piece]
        else:
            kind = {3: 0, 1: 1, 2: 2}[step]
            send, recv = y_send.at[kind, o, piece], y_recv.at[kind, o, piece]
        pltpu.make_async_remote_copy(
            src_ref=ref, dst_ref=ref, send_sem=send, recv_sem=recv, device_id=pair, device_id_type=MESH
        ).wait_recv()

    def y_start(o, *pieces):
        for a, b in pieces:
            need(o, 0, a)
            need(o, 0, b)
            y_copy(0, o, a).start()
            y_copy(1, o, b).start()

    def y_pass(o, *pieces):
        for piece in pieces:
            need(o, 3 if piece % 2 == 0 else 1, piece)
            y_copy(2, o, piece).start()

    def pair_copy(half, c):
        ref = (c, pl.ds(half * HALF, HALF))
        return pltpu.make_async_remote_copy(
            src_ref=to_pair.at[ref], dst_ref=from_pair.at[ref],
            send_sem=p_send.at[half, c], recv_sem=p_recv.at[half, c],
            device_id=pair, device_id_type=MESH,
        )

    def near_copy(half, c):
        rows = pl.ds(half * HALF, HALF)
        return pltpu.make_async_remote_copy(
            src_ref=near.at[c, rows], dst_ref=result.at[2 * c, rows],
            send_sem=n_send.at[half, c], recv_sem=n_recv.at[half, c],
            device_id=near_to, device_id_type=MESH,
        )

    def far_copy(half, c):
        rows = pl.ds(half * HALF, HALF)
        return pltpu.make_async_remote_copy(
            src_ref=far.at[c, rows], dst_ref=result.at[2 * c + 1, rows],
            send_sem=f_send.at[half, c], recv_sem=f_recv.at[half, c],
            device_id=far_to, device_id_type=MESH,
        )

    done = []

    def combine(half, c):
        rows = pl.ds(half * HALF, HALF)
        pair_copy(half, c).wait_recv()
        total = mine[c, rows] + from_pair[c, rows].astype(F32)
        pos = (side * 8 + c) * TOK + half * HALF + lax.broadcasted_iota(jnp.int32, (HALF, 1), 0)
        goal = jnp.zeros((HALF, 1), jnp.int32)
        edge = jnp.int32(0)
        for j in range(DOCS):
            goal = jnp.where(pos >= edge, dest_ref[0, j], goal)
            edge = edge + len_ref[0, j]
        far[c, rows] = jnp.where(goal == x, 0.0, total).astype(BF16)
        far_copy(half, c).start()
        kept = jnp.where(goal == x, total, 0.0).astype(BF16)

        @pl.when(stays)
        def _():
            result[2 * c, rows] = kept

        @pl.when(jnp.logical_not(stays))
        def _():
            near[c, rows] = kept
            near_copy(half, c).start()

    def project(*parts):
        for o, step, half in parts:
            for piece in (2 * half, 2 * half + 1):
                need(o, step, piece)
        places = [(place(o, step), pl.ds(half * HALF, HALF)) for o, step, half in parts]
        left = [jnp.concatenate([gathered[c, 0, rows], gathered[c, 1, rows]], axis=1) for c, rows in places]
        left = left[0] if len(left) == 1 else jnp.concatenate(left, axis=0)
        given = jnp.dot(left, w_ref[1 - keep], preferred_element_type=F32)
        for i, ((c, rows), (_, _, half)) in enumerate(zip(places, parts)):
            to_pair[c, rows] = given[i * HALF : (i + 1) * HALF].astype(BF16)
            pair_copy(half, c).start()
        kept = jnp.dot(left, w_ref[keep], preferred_element_type=F32)
        for i, (c, rows) in enumerate(places):
            mine[c, rows] = kept[i * HALF : (i + 1) * HALF]
        for (c, _), (_, _, half) in zip(places, parts):
            combine(half, c)
            done.append((half, c))

    def finish(half, c):
        pair_copy(half, c).wait_send()
        far_copy(half, c).wait()

        @pl.when(jnp.logical_not(stays))
        def _():
            near_copy(half, c).wait()

    w_spread(0)
    kv_rest(0)
    attend(0, 0)
    z_copy(0).start()
    y_copy(0, 0, 0).start()
    y_copy(1, 0, 0).start()
    w_spread(1)
    attend(1, 0)
    kv_rest(1)
    attend(0, 1)
    z_copy(1).start()
    z_copy(2).start()
    y_copy(0, 0, 1).start()
    y_copy(1, 0, 1).start()
    w_spread(2)
    w_pass(0)
    attend(1, 1)
    z_copy(3).start()
    w_spread(3)
    w_pass(1)
    y_start(1, (0, 0))
    y_pass(0, 0)
    y_start(1, (1, 1))
    y_pass(0, 1)
    w_pass(2)
    y_start(0, (2, 3), (3, 2))
    w_pass(3)
    y_pass(1, 0, 1)
    in_copies[5].wait()
    for part in range(4):
        wx_wait(1 - part % 2, part)
        wx_wait(2, part)
    project((0, 0, 0), (0, 0, 1))
    project((0, 1, 0), (0, 3, 0))
    y_start(1, (2, 3), (3, 2))
    project((1, 0, 0), (1, 0, 1))
    y_pass(0, 2, 3)
    project((1, 1, 0), (1, 3, 0))
    project((0, 2, 0), (1, 2, 0))
    y_pass(1, 2, 3)
    project((0, 1, 1), (0, 3, 1))
    for cond, copy in sends:

        @pl.when(cond)
        def _():
            copy.wait_send()

    for part in range(4):
        wz_copy(part).wait_send()
        z_copy(part).wait_send()
        for kind in range(3):
            wx_copy(kind, part).wait_send()
            y_copy(kind, 0, part).wait_send()
    project((1, 1, 1), (1, 3, 1))
    for half, c in done[:8]:
        finish(half, c)
    project((0, 2, 1))
    project((1, 2, 1))
    for part in range(4):
        for kind in range(3):
            y_copy(kind, 1, part).wait_send()
    for half, c in done[8:]:
        finish(half, c)


def shards(queries, keys, values, out_weight, doc_len, destination):
    dma = pltpu.SemaphoreType.DMA
    hbm = pl.BlockSpec(memory_space=pl.ANY)
    smem = pl.BlockSpec(memory_space=pltpu.SMEM)
    width = out_weight.shape[1]
    out = pl.pallas_call(
        kernel,
        out_shape=pltpu.VMEM((16, TOK, width), BF16),
        in_specs=[hbm, hbm, hbm, hbm, smem, smem],
        out_specs=pl.BlockSpec(memory_space=pltpu.VMEM),
        scratch_shapes=[
            pltpu.VMEM(queries.shape, BF16),
            pltpu.VMEM((2,) + out_weight.shape, BF16),
            pltpu.VMEM((WINDOW, 2, TOK, 2 * HEAD), BF16),
            pltpu.VMEM((8, 2, TOK, queries.shape[1] // 2), BF16),
            pltpu.VMEM((TOK, WINDOW * TOK), F32),
            pltpu.VMEM((8, TOK, width), F32),
            pltpu.VMEM((8, TOK, width), BF16),
            pltpu.VMEM((8, TOK, width), BF16),
            pltpu.VMEM((8, TOK, width), BF16),
            pltpu.VMEM((8, TOK, width), BF16),
            dma((6,)),
            dma((2, 11)),
            dma((2, WINDOW)),
            dma((4,)),
            dma((4,)),
            dma((3, 4)),
            dma((3, 4)),
            dma((4,)),
            dma((4,)),
            dma((3, 2, 4)),
            dma((3, 2, 4)),
            dma((2, 8)),
            dma((2, 8)),
            dma((2, 8)),
            dma((2, 8)),
            dma((2, 8)),
            dma((2, 8)),
        ],
        compiler_params=pltpu.CompilerParams(
            collective_id=0, has_side_effects=True, vmem_limit_bytes=56 * 2**20
        ),
        cost_estimate=pl.CostEstimate(flops=6 * 10**9, bytes_accessed=6 * 2**20, transcendentals=3 * 10**6),
    )(queries, keys, values, out_weight, doc_len, destination)
    return out.reshape(16 * TOK, width)


def solution(mesh):
    in_specs = (
        P(("dp", "seq"), "tensor"),
        P(("dp", "seq"), "tensor"),
        P(("dp", "seq"), "tensor"),
        P("tensor", "seq"),
        P("dp", None),
        P("dp", None),
    )
    out_specs = P(("dp", "tensor"), "seq")
    return jax.shard_map(shards, mesh=mesh, in_specs=in_specs, out_specs=out_specs, check_vma=False)
```

```python
import math

import jax
import jax.numpy as jnp
from jax import lax
from jax.experimental import pallas as pl
from jax.experimental.pallas import tpu as pltpu
from jax.sharding import PartitionSpec as P

MESH = pl.DeviceIdType.MESH
HEAD = 128
TOK = 128
DOCS = 16
WINDOW = 9
HALF = TOK // 2
BF16 = jnp.bfloat16
F32 = jnp.float32
NEG = -1e30


def kernel(
    q_hbm, k_hbm, v_hbm, w_hbm, len_ref, dest_ref, result,
    q_ref, w_ref, kv, gathered, bias, mine, to_pair, from_pair, near, far,
    in_sems, kv_send, kv_recv, wz_send, wz_recv, wx_send, wx_recv, z_send, z_recv, y_send, y_recv,
    p_send, p_recv, n_send, n_recv, f_send, f_recv,
):
    x = lax.axis_index("dp")
    s = lax.axis_index("seq")
    t = lax.axis_index("tensor")
    z = s // 4
    y = s % 4
    side = z // 2
    inner = z % 2
    stays = t == side
    keep = jnp.where(stays, 0, 1)
    s_other = (s + 8) % 16
    s_to = jnp.where(stays, s, s_other)
    t_to = jnp.where(stays, t, 1 - t)

    def at(zz, yy):
        return (x, (zz % 4) * 4 + yy % 4, t)

    pair = (x, s, 1 - t)
    near_to = (x, s_to, t_to)
    far_to = ((x + 2) % 4, s_to, t_to)

    in_copies = [
        pltpu.make_async_copy(
            ref.at[:, pl.ds(j * HEAD, HEAD)], kv.at[WINDOW - 1, j, :, pl.ds(n * HEAD, HEAD)], in_sems.at[2 * j + n]
        )
        for j in range(2)
        for n, ref in enumerate((k_hbm, v_hbm))
    ]
    in_copies += [
        pltpu.make_async_copy(q_hbm, q_ref, in_sems.at[4]),
        pltpu.make_async_copy(w_hbm, w_ref.at[0], in_sems.at[5]),
    ]
    for copy in in_copies:
        copy.start()

    barrier = pltpu.get_barrier_semaphore()
    others = [at(z, y + 1), at(z, y + 2), at(z, y + 3), at(z + 1, y), at(z + 2, y), at(z + 3, y), pair]
    others += [((x + 1) % 4, s, t), ((x + 2) % 4, s, t), ((x + 3) % 4, s, t)]
    others += [(x, s_other, 1 - t), ((x + 2) % 4, s_other, 1 - t)]
    for other in others:
        pl.semaphore_signal(barrier, inc=1, device_id=other, device_id_type=MESH)
    pl.semaphore_wait(barrier, len(others))

    def kv_copy(head, src, dst, index, device):
        return pltpu.make_async_remote_copy(
            src_ref=kv.at[src, head], dst_ref=kv.at[dst, head],
            send_sem=kv_send.at[head, index], recv_sem=kv_recv.at[head, dst],
            device_id=device, device_id_type=MESH,
        )

    def kv_wait(head, slot):
        @pl.when(s - 8 + slot >= 0)
        def _():
            pltpu.make_async_remote_copy(
                src_ref=kv.at[slot, head], dst_ref=kv.at[slot, head],
                send_sem=kv_send.at[head, 0], recv_sem=kv_recv.at[head, slot],
                device_id=pair, device_id_type=MESH,
            ).wait_recv()

    sends = []

    def kv_start(head, index, cond, src, dst, device):
        copy = kv_copy(head, src, dst, index, device)
        sends.append((cond, copy))

        @pl.when(cond)
        def _():
            copy.start()

    steps = [(n, (y + step) % 4) for n, step in enumerate((1, 3, 2))]

    def kv_column(head):
        in_copies[2 * head].wait()
        in_copies[2 * head + 1].wait()
        kv_start(head, 0, z < 3, 8, 4, at(z + 1, y))
        kv_start(head, 1, z < 2, 8, 0, at(z + 2, y))

    def kv_row(head):
        for n, yy in steps:
            kv_start(head, 2 + n, yy > y, 8, 8 - jnp.maximum(yy - y, 0), at(z, yy))

    def kv_relay(head):
        kv_wait(head, 4)
        for n, yy in steps:
            kv_start(head, 5 + n, z >= 1, 4, 4 - (yy - y), at(z, yy))
        kv_wait(head, 0)
        for n, yy in steps:
            kv_start(head, 8 + n, (z >= 2) & (yy < y), 0, jnp.maximum(y - yy, 0), at(z, yy))

    def kv_rest(head):
        for slot in (5, 6, 7, 1, 2, 3):
            kv_wait(head, slot)
        for slot in range(WINDOW - 1):

            @pl.when(s - 8 + slot < 0)
            def _():
                kv[slot, head] = jnp.zeros((TOK, 2 * HEAD), BF16)

    def w_rows(offset, part):
        return pl.ds((x + offset) % 4 * 512 + part * 128, 128)

    def wz_copy(part):
        return pltpu.make_async_remote_copy(
            src_ref=w_hbm.at[w_rows(0, part)], dst_ref=w_ref.at[1, w_rows(0, part)],
            send_sem=wz_send.at[part], recv_sem=wz_recv.at[part],
            device_id=at(z + 2, y), device_id_type=MESH,
        )

    def wx_copy(kind, part):
        origin = 0 if kind < 2 else (3 if part % 2 == 0 else 1)
        way = (1, 3, 1 if part % 2 == 0 else 3)[kind]
        ref = w_ref.at[1, w_rows(origin, part)]
        return pltpu.make_async_remote_copy(
            src_ref=ref, dst_ref=ref, send_sem=wx_send.at[kind, part], recv_sem=wx_recv.at[kind, part],
            device_id=((x + way) % 4, s, t), device_id_type=MESH,
        )

    def wx_wait(kind, part):
        offset = (3, 1, 2)[kind]
        ref = w_ref.at[1, w_rows(offset, part)]
        pltpu.make_async_remote_copy(
            src_ref=ref, dst_ref=ref, send_sem=wx_send.at[kind, part], recv_sem=wx_recv.at[kind, part],
            device_id=pair, device_id_type=MESH,
        ).wait_recv()

    def w_spread(part):
        wz_copy(part).wait_recv()
        wx_copy(0, part).start()
        wx_copy(1, part).start()

    def w_pass(part):
        wx_wait(part % 2, part)
        wx_copy(2, part).start()


    kv_column(0)
    kv_row(0)
    wz_copy(0).start()
    kv_column(1)
    for part in range(1, 4):
        wz_copy(part).start()
    kv_relay(0)
    kv_row(1)
    kv_relay(1)

    for half in range(2):
        q_pos = s * TOK + half * HALF + lax.broadcasted_iota(jnp.int32, (HALF, 1), 0)
        start = jnp.zeros((HALF, 1), jnp.int32)
        edge = jnp.int32(0)
        for j in range(DOCS):
            start = jnp.where(q_pos >= edge, edge, start)
            edge = edge + len_ref[0, j]
        k_pos = (s - 8) * TOK + lax.broadcasted_iota(jnp.int32, (HALF, WINDOW * TOK), 1)
        seen = (k_pos <= q_pos) & (k_pos >= start)
        bias[pl.ds(half * HALF, HALF), :] = jnp.where(seen, 0.0, NEG).astype(F32)

    in_copies[4].wait()

    own = inner * 4 + y
    factor = math.log2(math.e) / math.sqrt(HEAD)

    def attend(half, j):
        rows = pl.ds(half * HALF, HALF)
        key = kv[:, j, :, :HEAD].reshape(WINDOW * TOK, HEAD)
        value = kv[:, j, :, HEAD:].reshape(WINDOW * TOK, HEAD)
        query = jnp.concatenate([q_ref[rows, (j * 8 + h) * HEAD : (j * 8 + h + 1) * HEAD] for h in range(8)], axis=0)
        scores = lax.dot_general(query, key, (((1,), (1,)), ((), ())), preferred_element_type=F32)
        scores = (scores.reshape(8, HALF, WINDOW * TOK) + bias[rows, :][None]).reshape(8 * HALF, WINDOW * TOK)
        top = jnp.max(scores, axis=1, keepdims=True)
        expo = jnp.exp2((scores - top) * factor)
        total = jnp.sum(expo, axis=1, keepdims=True)
        blended = jnp.dot(expo.astype(BF16), value, preferred_element_type=F32) / total
        for h in range(8):
            gathered[own, j, rows, h * HEAD : (h + 1) * HEAD] = blended[h * HALF : (h + 1) * HALF].astype(BF16)

    def place(o, step):
        return (inner + o) % 2 * 4 + (y + step) % 4

    def piece_ref(o, step, piece):
        return gathered.at[place(o, step), piece % 2, pl.ds(piece // 2 * HALF, HALF)]

    def z_copy(piece):
        ref = piece_ref(0, 0, piece)
        return pltpu.make_async_remote_copy(
            src_ref=ref, dst_ref=ref, send_sem=z_send.at[piece], recv_sem=z_recv.at[piece],
            device_id=at(side * 2 + 1 - inner, y), device_id_type=MESH,
        )

    def y_copy(kind, o, piece):
        origin = 0 if kind < 2 else (3 if piece % 2 == 0 else 1)
        way = (1, 3, 1 if piece % 2 == 0 else 3)[kind]
        ref = piece_ref(o, origin, piece)
        return pltpu.make_async_remote_copy(
            src_ref=ref, dst_ref=ref, send_sem=y_send.at[kind, o, piece], recv_sem=y_recv.at[kind, o, piece],
            device_id=at(z, y + way), device_id_type=MESH,
        )

    arrived = set()

    def need(o, step, piece):
        if (o, step) == (0, 0) or (o, step, piece) in arrived:
            return
        arrived.add((o, step, piece))
        ref = piece_ref(o, step, piece)
        if step == 0:
            send, recv = z_send.at[piece], z_recv.at[piece]
        else:
            kind = {3: 0, 1: 1, 2: 2}[step]
            send, recv = y_send.at[kind, o, piece], y_recv.at[kind, o, piece]
        pltpu.make_async_remote_copy(
            src_ref=ref, dst_ref=ref, send_sem=send, recv_sem=recv, device_id=pair, device_id_type=MESH
        ).wait_recv()

    def y_start(o, *pieces):
        for a, b in pieces:
            need(o, 0, a)
            need(o, 0, b)
            y_copy(0, o, a).start()
            y_copy(1, o, b).start()

    def y_pass(o, *pieces):
        for piece in pieces:
            need(o, 3 if piece % 2 == 0 else 1, piece)
            y_copy(2, o, piece).start()

    def pair_copy(half, c):
        ref = (c, pl.ds(half * HALF, HALF))
        return pltpu.make_async_remote_copy(
            src_ref=to_pair.at[ref], dst_ref=from_pair.at[ref],
            send_sem=p_send.at[half, c], recv_sem=p_recv.at[half, c],
            device_id=pair, device_id_type=MESH,
        )

    def near_copy(half, c):
        rows = pl.ds(half * HALF, HALF)
        return pltpu.make_async_remote_copy(
            src_ref=near.at[c, rows], dst_ref=result.at[2 * c, rows],
            send_sem=n_send.at[half, c], recv_sem=n_recv.at[half, c],
            device_id=near_to, device_id_type=MESH,
        )

    def far_copy(half, c):
        rows = pl.ds(half * HALF, HALF)
        return pltpu.make_async_remote_copy(
            src_ref=far.at[c, rows], dst_ref=result.at[2 * c + 1, rows],
            send_sem=f_send.at[half, c], recv_sem=f_recv.at[half, c],
            device_id=far_to, device_id_type=MESH,
        )

    done = []

    def combine(half, c):
        rows = pl.ds(half * HALF, HALF)
        pos = (side * 8 + c) * TOK + half * HALF + lax.broadcasted_iota(jnp.int32, (HALF, 1), 0)
        goal = jnp.zeros((HALF, 1), jnp.int32)
        edge = jnp.int32(0)
        for j in range(DOCS):
            goal = jnp.where(pos >= edge, dest_ref[0, j], goal)
            edge = edge + len_ref[0, j]
        here = jnp.broadcast_to(goal == x, (HALF, far.shape[2]))
        pair_copy(half, c).wait_recv()
        total = mine[c, rows] + from_pair[c, rows].astype(F32)
        far[c, rows] = jnp.where(here, 0.0, total).astype(BF16)
        far_copy(half, c).start()
        kept = jnp.where(here, total, 0.0).astype(BF16)

        @pl.when(stays)
        def _():
            result[2 * c, rows] = kept

        @pl.when(jnp.logical_not(stays))
        def _():
            near[c, rows] = kept
            near_copy(half, c).start()

    def project(*parts):
        for o, step, half in parts:
            for piece in (2 * half, 2 * half + 1):
                need(o, step, piece)
        places = [(place(o, step), pl.ds(half * HALF, HALF)) for o, step, half in parts]
        left = [jnp.concatenate([gathered[c, 0, rows], gathered[c, 1, rows]], axis=1) for c, rows in places]
        left = left[0] if len(left) == 1 else jnp.concatenate(left, axis=0)
        given = jnp.dot(left, w_ref[1 - keep], preferred_element_type=F32)
        for i, ((c, rows), (_, _, half)) in enumerate(zip(places, parts)):
            to_pair[c, rows] = given[i * HALF : (i + 1) * HALF].astype(BF16)
            pair_copy(half, c).start()
        kept = jnp.dot(left, w_ref[keep], preferred_element_type=F32)
        for i, (c, rows) in enumerate(places):
            mine[c, rows] = kept[i * HALF : (i + 1) * HALF]
        for (c, _), (_, _, half) in zip(places, parts):
            combine(half, c)
            done.append((half, c))

    def finish(half, c):
        pair_copy(half, c).wait_send()
        far_copy(half, c).wait()

        @pl.when(jnp.logical_not(stays))
        def _():
            near_copy(half, c).wait()

    w_spread(0)
    kv_rest(0)
    attend(0, 0)
    z_copy(0).start()
    y_copy(0, 0, 0).start()
    y_copy(1, 0, 0).start()
    w_spread(1)
    attend(1, 0)
    kv_rest(1)
    attend(0, 1)
    z_copy(1).start()
    z_copy(2).start()
    y_copy(0, 0, 1).start()
    y_copy(1, 0, 1).start()
    w_spread(2)
    w_pass(0)
    attend(1, 1)
    z_copy(3).start()
    w_spread(3)
    w_pass(1)
    y_start(1, (0, 0))
    y_pass(0, 0)
    y_start(1, (1, 1))
    y_pass(0, 1)
    w_pass(2)
    y_start(0, (2, 3), (3, 2))
    w_pass(3)
    y_pass(1, 0, 1)
    in_copies[5].wait()
    for part in range(4):
        wx_wait(1 - part % 2, part)
        wx_wait(2, part)
    project((0, 0, 0), (0, 0, 1))
    project((0, 1, 0), (0, 3, 0))
    y_start(1, (2, 3), (3, 2))
    project((1, 0, 0), (1, 0, 1))
    y_pass(0, 2, 3)
    project((1, 1, 0), (1, 3, 0))
    project((0, 2, 0), (1, 2, 0))
    project((0, 1, 1), (0, 3, 1))
    y_pass(1, 2, 3)
    for cond, copy in sends:

        @pl.when(cond)
        def _():
            copy.wait_send()

    for part in range(4):
        wz_copy(part).wait_send()
        z_copy(part).wait_send()
        for kind in range(3):
            wx_copy(kind, part).wait_send()
            y_copy(kind, 0, part).wait_send()
    project((1, 1, 1), (1, 3, 1))
    project((0, 2, 1))
    project((1, 2, 1))
    for part in range(4):
        for kind in range(3):
            y_copy(kind, 1, part).wait_send()
    for half, c in done:
        finish(half, c)


def shards(queries, keys, values, out_weight, doc_len, destination):
    dma = pltpu.SemaphoreType.DMA
    hbm = pl.BlockSpec(memory_space=pl.ANY)
    smem = pl.BlockSpec(memory_space=pltpu.SMEM)
    width = out_weight.shape[1]
    out = pl.pallas_call(
        kernel,
        out_shape=pltpu.VMEM((16, TOK, width), BF16),
        in_specs=[hbm, hbm, hbm, hbm, smem, smem],
        out_specs=pl.BlockSpec(memory_space=pltpu.VMEM),
        scratch_shapes=[
            pltpu.VMEM(queries.shape, BF16),
            pltpu.VMEM((2,) + out_weight.shape, BF16),
            pltpu.VMEM((WINDOW, 2, TOK, 2 * HEAD), BF16),
            pltpu.VMEM((8, 2, TOK, queries.shape[1] // 2), BF16),
            pltpu.VMEM((TOK, WINDOW * TOK), F32),
            pltpu.VMEM((8, TOK, width), F32),
            pltpu.VMEM((8, TOK, width), BF16),
            pltpu.VMEM((8, TOK, width), BF16),
            pltpu.VMEM((8, TOK, width), BF16),
            pltpu.VMEM((8, TOK, width), BF16),
            dma((6,)),
            dma((2, 11)),
            dma((2, WINDOW)),
            dma((4,)),
            dma((4,)),
            dma((3, 4)),
            dma((3, 4)),
            dma((4,)),
            dma((4,)),
            dma((3, 2, 4)),
            dma((3, 2, 4)),
            dma((2, 8)),
            dma((2, 8)),
            dma((2, 8)),
            dma((2, 8)),
            dma((2, 8)),
            dma((2, 8)),
        ],
        compiler_params=pltpu.CompilerParams(
            collective_id=0, has_side_effects=True, vmem_limit_bytes=56 * 2**20
        ),
        cost_estimate=pl.CostEstimate(flops=6 * 10**9, bytes_accessed=6 * 2**20, transcendentals=3 * 10**6),
    )(queries, keys, values, out_weight, doc_len, destination)
    return out.reshape(16 * TOK, width)


def solution(mesh):
    in_specs = (
        P(("dp", "seq"), "tensor"),
        P(("dp", "seq"), "tensor"),
        P(("dp", "seq"), "tensor"),
        P("tensor", "seq"),
        P("dp", None),
        P("dp", None),
    )
    out_specs = P(("dp", "tensor"), "seq")
    return jax.shard_map(shards, mesh=mesh, in_specs=in_specs, out_specs=out_specs, check_vma=False)
```

```python
import math

import jax
import jax.numpy as jnp
from jax import lax
from jax.experimental import pallas as pl
from jax.experimental.pallas import tpu as pltpu
from jax.sharding import PartitionSpec as P

MESH = pl.DeviceIdType.MESH
HEAD = 128
TOK = 128
DOCS = 16
WINDOW = 9
HALF = TOK // 2
BF16 = jnp.bfloat16
F32 = jnp.float32
NEG = -1e30


def kernel(
    q_hbm, k_hbm, v_hbm, w_hbm, len_ref, dest_ref, result,
    q_ref, w_ref, kv, gathered, bias, mine, to_pair, from_pair, near, far,
    in_sems, kv_send, kv_recv, wz_send, wz_recv, wx_send, wx_recv, z_send, z_recv, y_send, y_recv,
    p_send, p_recv, n_send, n_recv, f_send, f_recv,
):
    x = lax.axis_index("dp")
    s = lax.axis_index("seq")
    t = lax.axis_index("tensor")
    z = s // 4
    y = s % 4
    side = z // 2
    inner = z % 2
    stays = t == side
    keep = jnp.where(stays, 0, 1)
    s_other = (s + 8) % 16
    s_to = jnp.where(stays, s, s_other)
    t_to = jnp.where(stays, t, 1 - t)

    def at(zz, yy):
        return (x, (zz % 4) * 4 + yy % 4, t)

    pair = (x, s, 1 - t)
    near_to = (x, s_to, t_to)
    far_to = ((x + 2) % 4, s_to, t_to)

    in_copies = [
        pltpu.make_async_copy(
            ref.at[:, pl.ds(j * HEAD, HEAD)], kv.at[WINDOW - 1, j, :, pl.ds(n * HEAD, HEAD)], in_sems.at[2 * j + n]
        )
        for j in range(2)
        for n, ref in enumerate((k_hbm, v_hbm))
    ]
    in_copies += [
        pltpu.make_async_copy(q_hbm, q_ref, in_sems.at[4]),
        pltpu.make_async_copy(w_hbm, w_ref.at[0], in_sems.at[5]),
    ]
    for copy in in_copies:
        copy.start()

    barrier = pltpu.get_barrier_semaphore()
    others = [at(z, y + 1), at(z, y + 2), at(z, y + 3), at(z + 1, y), at(z + 2, y), at(z + 3, y), pair]
    others += [((x + 1) % 4, s, t), ((x + 2) % 4, s, t), ((x + 3) % 4, s, t)]
    others += [(x, s_other, 1 - t), ((x + 2) % 4, s_other, 1 - t)]
    for other in others:
        pl.semaphore_signal(barrier, inc=1, device_id=other, device_id_type=MESH)
    pl.semaphore_wait(barrier, len(others))

    def kv_copy(head, src, dst, index, device):
        return pltpu.make_async_remote_copy(
            src_ref=kv.at[src, head], dst_ref=kv.at[dst, head],
            send_sem=kv_send.at[head, index], recv_sem=kv_recv.at[head, dst],
            device_id=device, device_id_type=MESH,
        )

    def kv_wait(head, slot):
        @pl.when(s - 8 + slot >= 0)
        def _():
            pltpu.make_async_remote_copy(
                src_ref=kv.at[slot, head], dst_ref=kv.at[slot, head],
                send_sem=kv_send.at[head, 0], recv_sem=kv_recv.at[head, slot],
                device_id=pair, device_id_type=MESH,
            ).wait_recv()

    sends = []

    def kv_start(head, index, cond, src, dst, device):
        copy = kv_copy(head, src, dst, index, device)
        sends.append((cond, copy))

        @pl.when(cond)
        def _():
            copy.start()

    steps = [(n, (y + step) % 4) for n, step in enumerate((1, 3, 2))]

    def kv_column(head):
        in_copies[2 * head].wait()
        in_copies[2 * head + 1].wait()
        kv_start(head, 0, z < 3, 8, 4, at(z + 1, y))
        kv_start(head, 1, z < 2, 8, 0, at(z + 2, y))

    def kv_row(head):
        for n, yy in steps:
            kv_start(head, 2 + n, yy > y, 8, 8 - jnp.maximum(yy - y, 0), at(z, yy))

    def kv_relay(head):
        kv_wait(head, 4)
        for n, yy in steps:
            kv_start(head, 5 + n, z >= 1, 4, 4 - (yy - y), at(z, yy))
        kv_wait(head, 0)
        for n, yy in steps:
            kv_start(head, 8 + n, (z >= 2) & (yy < y), 0, jnp.maximum(y - yy, 0), at(z, yy))

    def kv_rest(head):
        for slot in (5, 6, 7, 1, 2, 3):
            kv_wait(head, slot)
        for slot in range(WINDOW - 1):

            @pl.when(s - 8 + slot < 0)
            def _():
                kv[slot, head] = jnp.zeros((TOK, 2 * HEAD), BF16)

    def w_rows(offset, part):
        return pl.ds((x + offset) % 4 * 512 + part * 128, 128)

    def wz_copy(part):
        return pltpu.make_async_remote_copy(
            src_ref=w_hbm.at[w_rows(0, part)], dst_ref=w_ref.at[1, w_rows(0, part)],
            send_sem=wz_send.at[part], recv_sem=wz_recv.at[part],
            device_id=at(z + 2, y), device_id_type=MESH,
        )

    def wx_copy(kind, part):
        origin = 0 if kind < 2 else (3 if part % 2 == 0 else 1)
        way = (1, 3, 1 if part % 2 == 0 else 3)[kind]
        ref = w_ref.at[1, w_rows(origin, part)]
        return pltpu.make_async_remote_copy(
            src_ref=ref, dst_ref=ref, send_sem=wx_send.at[kind, part], recv_sem=wx_recv.at[kind, part],
            device_id=((x + way) % 4, s, t), device_id_type=MESH,
        )

    def wx_wait(kind, part):
        offset = (3, 1, 2)[kind]
        ref = w_ref.at[1, w_rows(offset, part)]
        pltpu.make_async_remote_copy(
            src_ref=ref, dst_ref=ref, send_sem=wx_send.at[kind, part], recv_sem=wx_recv.at[kind, part],
            device_id=pair, device_id_type=MESH,
        ).wait_recv()

    def w_spread(part):
        wz_copy(part).wait_recv()
        wx_copy(0, part).start()
        wx_copy(1, part).start()

    def w_pass(part):
        wx_wait(part % 2, part)
        wx_copy(2, part).start()


    kv_column(0)
    kv_row(0)
    kv_column(1)
    for part in range(4):
        wz_copy(part).start()
    kv_relay(0)
    kv_row(1)
    kv_relay(1)

    for half in range(2):
        q_pos = s * TOK + half * HALF + lax.broadcasted_iota(jnp.int32, (HALF, 1), 0)
        start = jnp.zeros((HALF, 1), jnp.int32)
        edge = jnp.int32(0)
        for j in range(DOCS):
            start = jnp.where(q_pos >= edge, edge, start)
            edge = edge + len_ref[0, j]
        k_pos = (s - 8) * TOK + lax.broadcasted_iota(jnp.int32, (HALF, WINDOW * TOK), 1)
        seen = (k_pos <= q_pos) & (k_pos >= start)
        bias[pl.ds(half * HALF, HALF), :] = jnp.where(seen, 0.0, NEG).astype(F32)

    in_copies[4].wait()

    own = inner * 4 + y
    factor = math.log2(math.e) / math.sqrt(HEAD)

    def attend(half, j):
        rows = pl.ds(half * HALF, HALF)
        key = kv[:, j, :, :HEAD].reshape(WINDOW * TOK, HEAD)
        value = kv[:, j, :, HEAD:].reshape(WINDOW * TOK, HEAD)
        query = jnp.concatenate([q_ref[rows, (j * 8 + h) * HEAD : (j * 8 + h + 1) * HEAD] for h in range(8)], axis=0)
        scores = lax.dot_general(query, key, (((1,), (1,)), ((), ())), preferred_element_type=F32)
        scores = (scores.reshape(8, HALF, WINDOW * TOK) + bias[rows, :][None]).reshape(8 * HALF, WINDOW * TOK)
        top = jnp.max(scores, axis=1, keepdims=True)
        expo = jnp.exp2((scores - top) * factor)
        total = jnp.sum(expo, axis=1, keepdims=True)
        blended = jnp.dot(expo.astype(BF16), value, preferred_element_type=F32) / total
        for h in range(8):
            gathered[own, j, rows, h * HEAD : (h + 1) * HEAD] = blended[h * HALF : (h + 1) * HALF].astype(BF16)

    def place(o, step):
        return (inner + o) % 2 * 4 + (y + step) % 4

    def piece_ref(o, step, piece):
        return gathered.at[place(o, step), piece % 2, pl.ds(piece // 2 * HALF, HALF)]

    def z_copy(piece):
        ref = piece_ref(0, 0, piece)
        return pltpu.make_async_remote_copy(
            src_ref=ref, dst_ref=ref, send_sem=z_send.at[piece], recv_sem=z_recv.at[piece],
            device_id=at(side * 2 + 1 - inner, y), device_id_type=MESH,
        )

    def y_copy(kind, o, piece):
        origin = 0 if kind < 2 else (3 if piece % 2 == 0 else 1)
        way = (1, 3, 1 if piece % 2 == 0 else 3)[kind]
        ref = piece_ref(o, origin, piece)
        return pltpu.make_async_remote_copy(
            src_ref=ref, dst_ref=ref, send_sem=y_send.at[kind, o, piece], recv_sem=y_recv.at[kind, o, piece],
            device_id=at(z, y + way), device_id_type=MESH,
        )

    arrived = set()

    def need(o, step, piece):
        if (o, step) == (0, 0) or (o, step, piece) in arrived:
            return
        arrived.add((o, step, piece))
        ref = piece_ref(o, step, piece)
        if step == 0:
            send, recv = z_send.at[piece], z_recv.at[piece]
        else:
            kind = {3: 0, 1: 1, 2: 2}[step]
            send, recv = y_send.at[kind, o, piece], y_recv.at[kind, o, piece]
        pltpu.make_async_remote_copy(
            src_ref=ref, dst_ref=ref, send_sem=send, recv_sem=recv, device_id=pair, device_id_type=MESH
        ).wait_recv()

    def y_start(o, *pieces):
        for a, b in pieces:
            need(o, 0, a)
            need(o, 0, b)
            y_copy(0, o, a).start()
            y_copy(1, o, b).start()

    def y_pass(o, *pieces):
        for piece in pieces:
            need(o, 3 if piece % 2 == 0 else 1, piece)
            y_copy(2, o, piece).start()

    def pair_copy(half, c):
        ref = (c, pl.ds(half * HALF, HALF))
        return pltpu.make_async_remote_copy(
            src_ref=to_pair.at[ref], dst_ref=from_pair.at[ref],
            send_sem=p_send.at[half, c], recv_sem=p_recv.at[half, c],
            device_id=pair, device_id_type=MESH,
        )

    def near_copy(half, c):
        rows = pl.ds(half * HALF, HALF)
        return pltpu.make_async_remote_copy(
            src_ref=near.at[c, rows], dst_ref=result.at[2 * c, rows],
            send_sem=n_send.at[half, c], recv_sem=n_recv.at[half, c],
            device_id=near_to, device_id_type=MESH,
        )

    def far_copy(half, c):
        rows = pl.ds(half * HALF, HALF)
        return pltpu.make_async_remote_copy(
            src_ref=far.at[c, rows], dst_ref=result.at[2 * c + 1, rows],
            send_sem=f_send.at[half, c], recv_sem=f_recv.at[half, c],
            device_id=far_to, device_id_type=MESH,
        )

    done = []

    def combine(half, c):
        rows = pl.ds(half * HALF, HALF)
        pair_copy(half, c).wait_recv()
        total = mine[c, rows] + from_pair[c, rows].astype(F32)
        pos = (side * 8 + c) * TOK + half * HALF + lax.broadcasted_iota(jnp.int32, (HALF, 1), 0)
        goal = jnp.zeros((HALF, 1), jnp.int32)
        edge = jnp.int32(0)
        for j in range(DOCS):
            goal = jnp.where(pos >= edge, dest_ref[0, j], goal)
            edge = edge + len_ref[0, j]
        far[c, rows] = jnp.where(goal == x, 0.0, total).astype(BF16)
        far_copy(half, c).start()
        kept = jnp.where(goal == x, total, 0.0).astype(BF16)

        @pl.when(stays)
        def _():
            result[2 * c, rows] = kept

        @pl.when(jnp.logical_not(stays))
        def _():
            near[c, rows] = kept
            near_copy(half, c).start()

    def project(*parts):
        for o, step, half in parts:
            for piece in (2 * half, 2 * half + 1):
                need(o, step, piece)
        places = [(place(o, step), pl.ds(half * HALF, HALF)) for o, step, half in parts]
        left = [jnp.concatenate([gathered[c, 0, rows], gathered[c, 1, rows]], axis=1) for c, rows in places]
        left = left[0] if len(left) == 1 else jnp.concatenate(left, axis=0)
        given = jnp.dot(left, w_ref[1 - keep], preferred_element_type=F32)
        for i, ((c, rows), (_, _, half)) in enumerate(zip(places, parts)):
            to_pair[c, rows] = given[i * HALF : (i + 1) * HALF].astype(BF16)
            pair_copy(half, c).start()
        kept = jnp.dot(left, w_ref[keep], preferred_element_type=F32)
        for i, (c, rows) in enumerate(places):
            mine[c, rows] = kept[i * HALF : (i + 1) * HALF]
        for (c, _), (_, _, half) in zip(places, parts):
            combine(half, c)
            done.append((half, c))

    def finish(half, c):
        pair_copy(half, c).wait_send()
        far_copy(half, c).wait()

        @pl.when(jnp.logical_not(stays))
        def _():
            near_copy(half, c).wait()

    w_spread(0)
    kv_rest(0)
    attend(0, 0)
    z_copy(0).start()
    y_copy(0, 0, 0).start()
    y_copy(1, 0, 0).start()
    w_spread(1)
    attend(1, 0)
    kv_rest(1)
    attend(0, 1)
    z_copy(1).start()
    z_copy(2).start()
    y_copy(0, 0, 1).start()
    y_copy(1, 0, 1).start()
    w_spread(2)
    w_pass(0)
    attend(1, 1)
    z_copy(3).start()
    w_spread(3)
    w_pass(1)
    y_start(1, (0, 0))
    y_pass(0, 0)
    y_start(1, (1, 1))
    y_pass(0, 1)
    w_pass(2)
    y_start(0, (2, 3), (3, 2))
    w_pass(3)
    y_pass(1, 0, 1)
    in_copies[5].wait()
    for part in range(4):
        wx_wait(1 - part % 2, part)
        wx_wait(2, part)
    project((0, 0, 0), (0, 0, 1))
    project((0, 1, 0), (0, 3, 0))
    y_start(1, (2, 3), (3, 2))
    project((1, 0, 0), (1, 0, 1))
    y_pass(0, 2, 3)
    project((1, 1, 0), (1, 3, 0))
    project((0, 2, 0), (1, 2, 0))
    y_pass(1, 2, 3)
    project((0, 1, 1), (0, 3, 1))
    for cond, copy in sends:

        @pl.when(cond)
        def _():
            copy.wait_send()

    for part in range(4):
        wz_copy(part).wait_send()
        z_copy(part).wait_send()
        for kind in range(3):
            wx_copy(kind, part).wait_send()
            y_copy(kind, 0, part).wait_send()
    project((1, 1, 1), (1, 3, 1))
    for half, c in done[:8]:
        finish(half, c)
    project((0, 2, 1))
    project((1, 2, 1))
    for part in range(4):
        for kind in range(3):
            y_copy(kind, 1, part).wait_send()
    for half, c in done[8:]:
        finish(half, c)


def shards(queries, keys, values, out_weight, doc_len, destination):
    dma = pltpu.SemaphoreType.DMA
    hbm = pl.BlockSpec(memory_space=pl.ANY)
    smem = pl.BlockSpec(memory_space=pltpu.SMEM)
    width = out_weight.shape[1]
    out = pl.pallas_call(
        kernel,
        out_shape=pltpu.VMEM((16, TOK, width), BF16),
        in_specs=[hbm, hbm, hbm, hbm, smem, smem],
        out_specs=pl.BlockSpec(memory_space=pltpu.VMEM),
        scratch_shapes=[
            pltpu.VMEM(queries.shape, BF16),
            pltpu.VMEM((2,) + out_weight.shape, BF16),
            pltpu.VMEM((WINDOW, 2, TOK, 2 * HEAD), BF16),
            pltpu.VMEM((8, 2, TOK, queries.shape[1] // 2), BF16),
            pltpu.VMEM((TOK, WINDOW * TOK), F32),
            pltpu.VMEM((8, TOK, width), F32),
            pltpu.VMEM((8, TOK, width), BF16),
            pltpu.VMEM((8, TOK, width), BF16),
            pltpu.VMEM((8, TOK, width), BF16),
            pltpu.VMEM((8, TOK, width), BF16),
            dma((6,)),
            dma((2, 11)),
            dma((2, WINDOW)),
            dma((4,)),
            dma((4,)),
            dma((3, 4)),
            dma((3, 4)),
            dma((4,)),
            dma((4,)),
            dma((3, 2, 4)),
            dma((3, 2, 4)),
            dma((2, 8)),
            dma((2, 8)),
            dma((2, 8)),
            dma((2, 8)),
            dma((2, 8)),
            dma((2, 8)),
        ],
        compiler_params=pltpu.CompilerParams(
            collective_id=0, has_side_effects=True, vmem_limit_bytes=56 * 2**20
        ),
        cost_estimate=pl.CostEstimate(flops=6 * 10**9, bytes_accessed=6 * 2**20, transcendentals=3 * 10**6),
    )(queries, keys, values, out_weight, doc_len, destination)
    return out.reshape(16 * TOK, width)


def solution(mesh):
    in_specs = (
        P(("dp", "seq"), "tensor"),
        P(("dp", "seq"), "tensor"),
        P(("dp", "seq"), "tensor"),
        P("tensor", "seq"),
        P("dp", None),
        P("dp", None),
    )
    out_specs = P(("dp", "tensor"), "seq")
    return jax.shard_map(shards, mesh=mesh, in_specs=in_specs, out_specs=out_specs, check_vma=False)
```
